128 devices in a mesh: dp: 64 (over x, z, y_lo, core), tensor: 2 (over y_hi).
Axes of the slice: x: 4, y: 4 (y_hi: 2, y_lo: 2; y = y_hi * 2 + y_lo), z: 4, core: 2. Of those that a mesh axis runs over, the one named last changes fastest.
Arguments:
- tokens: bfloat16 [32768, 1024], P(('dp', 'tensor')), may hold values from -6 to 6
- w_qkv: bfloat16 [1, 1024, 3, 1024], P(None, 'dp', None, 'tensor'), may hold values from -0.25 to 0.25
- b_qv: bfloat16 [1, 2, 1024], replicated, may hold values from -3 to 3
- w_out: bfloat16 [1, 1024, 1024], P(None, 'tensor', 'dp'), may hold values from -1 to 1
- b_out: bfloat16 [1, 1024], replicated, may hold values from -3 to 3
- gain_attn: bfloat16 [1, 1024], replicated, may hold values from 0.5 to 1.5
- shift_attn: bfloat16 [1, 1024], replicated, may hold values from -3 to 3
- w_in: bfloat16 [1, 1024, 4096], P(None, 'dp', 'tensor'), may hold values from -0.1875 to 0.1875
- b_in: bfloat16 [1, 4096], replicated, may hold values from -3 to 3
- w_back: bfloat16 [1, 4096, 1024], P(None, 'tensor', 'dp'), may hold values from -0.125 to 0.125
- b_back: bfloat16 [1, 1024], replicated, may hold values from -3 to 3
- gain_ffn: bfloat16 [1, 1024], replicated, may hold values from 0.5 to 1.5
- shift_ffn: bfloat16 [1, 1024], replicated, may hold values from -3 to 3
- cotangent: bfloat16 [32768, 1024], P(('dp', 'tensor')), may hold values from -6 to 6
Outputs:
- encoded: bfloat16 [32768, 1024], P(('dp', 'tensor'))
- grad_tokens: float32 [32768, 1024], P(('dp', 'tensor'))
- grad_w_qkv: float32 [1, 1024, 3, 1024], P(None, 'dp', None, 'tensor')
- grad_b_qv: float32 [1, 2, 1024], replicated
- grad_w_out: float32 [1, 1024, 1024], P(None, 'tensor', 'dp')
- grad_b_out: float32 [1, 1024], replicated
- grad_gain_attn: float32 [1, 1024], replicated
- grad_shift_attn: float32 [1, 1024], replicated
- grad_w_in: float32 [1, 1024, 4096], P(None, 'dp', 'tensor')
- grad_b_in: float32 [1, 4096], replicated
- grad_w_back: float32 [1, 4096, 1024], P(None, 'tensor', 'dp')
- grad_b_back: float32 [1, 1024], replicated
- grad_gain_ffn: float32 [1, 1024], replicated
- grad_shift_ffn: float32 [1, 1024], replicated
The draws below stay inside these ranges and needn't reach their ends.
All inputs are finite; a program needn't handle non-finite values.
Results may differ from the reference program's by a relative error of at most 0.019.
Values may be sent and summed in bfloat16 or wider, within the bound.
A program may use at most 128 MiB of HBM per device.

```python
import jax
import jax.numpy as jnp
from jax import lax

D = 1024
HEADS = 16
HD = 64
FF = 4096
SEQ = 512
LAYERS = 1
TOKENS = 32768
N_DP = 64


def shard_levels(key, shape, split, least, top_value):
    level, own = 1.0, jax.random.fold_in(key, 6)
    for axis_at, parts in split:
        heights = jnp.exp(jax.random.uniform(jax.random.fold_in(own, axis_at), (parts,), jnp.float32, least / len(split), top_value / len(split)))
        level = level * jnp.repeat(heights, shape[axis_at] // parts).reshape([-1 if axis == axis_at else 1 for axis in range(len(shape))])
    return level


def normal_values(own_key, dims, spread, limit, cuts=(), kind=jnp.bfloat16):
    loudness = shard_levels(own_key, dims, cuts, -0.22, 0.18) if cuts else 1.0
    result = jax.random.normal(own_key, dims, jnp.float32) * spread * loudness
    return jnp.minimum(jnp.maximum(result, -limit), limit).astype(kind)


def setup_inputs(seed: int = 0) -> dict:
    key_list = jax.random.split(jax.random.key(seed), 15)
    tokens = normal_values(key_list[0], (TOKENS, D), 1.0, 6.0, ((0, 128),))
    w_qkv = normal_values(key_list[1], (LAYERS, D, 3, D), (D // 2) ** -0.5, 0.25, ((1, 64), (3, 2)))
    b_qv = normal_values(key_list[2], (LAYERS, 2, D), 0.5, 3.0)
    w_out = normal_values(key_list[3], (LAYERS, D, D), (D // 32) ** -0.5, 1.0, ((1, 2), (2, 64)))
    b_out = normal_values(key_list[4], (LAYERS, D), 0.5, 3.0)
    gain_attn = jnp.clip(1.0 + 0.1 * jax.random.normal(key_list[5], (LAYERS, D), jnp.float32), 0.5, 1.5).astype(jnp.bfloat16)
    shift_attn = normal_values(key_list[6], (LAYERS, D), 0.5, 3.0)
    w_in = normal_values(key_list[7], (LAYERS, D, FF), D ** -0.5, 0.1875, ((1, 64), (2, 2)))
    b_in = normal_values(key_list[8], (LAYERS, FF), 0.5, 3.0)
    w_back = normal_values(key_list[9], (LAYERS, FF, D), (FF // 2) ** -0.5, 0.125, ((1, 2), (2, 64)))
    b_back = normal_values(key_list[10], (LAYERS, D), 0.5, 3.0)
    gain_ffn = jnp.clip(1.0 + 0.1 * jax.random.normal(key_list[11], (LAYERS, D), jnp.float32), 0.5, 1.5).astype(jnp.bfloat16)
    shift_ffn = normal_values(key_list[12], (LAYERS, D), 0.5, 3.0)
    cotangent = normal_values(key_list[13], (TOKENS, D), 1.0, 6.0, ((0, 128),))
    return {"tokens": tokens, "w_qkv": w_qkv, "b_qv": b_qv, "w_out": w_out, "b_out": b_out, "gain_attn": gain_attn, "shift_attn": shift_attn, "w_in": w_in, "b_in": b_in, "w_back": w_back, "b_back": b_back, "gain_ffn": gain_ffn, "shift_ffn": shift_ffn, "cotangent": cotangent}


@jax.custom_vjp
def low(v):
    return lax.optimization_barrier(v.astype(jnp.bfloat16)).astype(jnp.float32)

@jax.custom_vjp
def low_back(v):
    return v

def low_keep(v):
    return (low(v), None)

def low_pass(kept, grad):
    return (grad,)

def back_keep(v):
    return (v, None)

def back_low(kept, grad):
    return (low(grad),)
low.defvjp(low_keep, low_pass)
low_back.defvjp(back_keep, back_low)
precise = lax.Precision.HIGHEST
epsilon = 1e-05
root_half = 0.7071067811865476

def matmul_high(left, right):
    return jnp.dot(left, right, precision=precise)

def gelu_exact(values):
    return 0.5 * values * (1.0 + lax.erf(values * root_half))

def layer_norm(stream, gain, shift):
    center = stream - lax.optimization_barrier(jnp.mean(stream, axis=-1, keepdims=True))
    variance = lax.optimization_barrier(jnp.mean(center * center, axis=-1, keepdims=True))
    return center * lax.rsqrt(variance + epsilon) * gain + shift

def attention(query, keys, values):
    length = query.shape[0]
    query_heads = query.reshape(length, HEADS, HD)
    key_heads = keys.reshape(length, HEADS, HD)
    value_heads = values.reshape(length, HEADS, HD)
    scores = low_back(jnp.einsum('shd,thd->hst', query_heads, key_heads, precision=precise) * HD ** (-0.5))
    weights = jax.nn.softmax(scores, axis=-1)
    mixed = jnp.einsum('hst,thd->shd', low(weights), value_heads, precision=precise)
    return mixed.reshape(length, HEADS * HD)

def encoder_layer(stream, layer_weights):
    w_qkv, b_qv, w_out, b_out, gain_attn, shift_attn, w_in, b_in, w_back, b_back, gain_ffn, shift_ffn = layer_weights
    stream_low = low(stream)
    projected = jnp.einsum('sd,dcf->scf', stream_low, w_qkv, precision=precise)
    query = low(low_back(projected[:, 0] + b_qv[0]))
    keys = low(low_back(projected[:, 1]))
    values = low(low_back(projected[:, 2] + b_qv[1]))
    mixed = low(low_back(attention(query, keys, values)))
    attended = low_back(matmul_high(mixed, w_out)) + b_out
    hidden = layer_norm(stream + attended, gain_attn, shift_attn)
    hidden_low = low(hidden)
    upward = low_back(matmul_high(hidden_low, w_in) + b_in)
    activated = low(gelu_exact(upward))
    downward = low_back(matmul_high(activated, w_back)) + b_back
    return layer_norm(hidden + downward, gain_ffn, shift_ffn)

def reference(tokens, w_qkv, b_qv, w_out, b_out, gain_attn, shift_attn, w_in, b_in, w_back, b_back, gain_ffn, shift_ffn, cotangent):
    params = tuple((array.astype(jnp.float32) for array in (w_qkv, b_qv, w_out, b_out, gain_attn, shift_attn, w_in, b_in, w_back, b_back, gain_ffn, shift_ffn)))

    def network(stream, all_weights):
        for layer_index in range(LAYERS):
            stream = encoder_layer(stream, tuple((weight[layer_index] for weight in all_weights)))
        return stream

    def per_sequence(totals, inputs):
        sequence, seq_cotangent = inputs
        output, pullback = jax.vjp(network, sequence, params)
        grad_stream, grad_params = pullback(seq_cotangent)
        totals = jax.tree.map(jnp.add, totals, grad_params)
        return (totals, (output, grad_stream))
    initial = tuple((jnp.zeros_like(weight) for weight in params))
    sequences = tokens.astype(jnp.float32).reshape(N_DP, SEQ, D)
    cotangents = cotangent.astype(jnp.float32).reshape(N_DP, SEQ, D)
    gradients, (outputs, grad_stream) = lax.scan(per_sequence, initial, (sequences, cotangents))
    return (outputs.reshape(TOKENS, D).astype(jnp.bfloat16), grad_stream.reshape(TOKENS, D), gradients[0], gradients[1], gradients[2], gradients[3], gradients[4], gradients[5], gradients[6], gradients[7], gradients[8], gradients[9], gradients[10], gradients[11])
```

```python
import jax
import jax.numpy as jnp
from jax import lax
from jax.experimental import pallas as pl
from jax.experimental.pallas import tpu as pltpu
from jax.sharding import PartitionSpec as P

F32 = jnp.float32
BF16 = jnp.bfloat16
MESH = pl.DeviceIdType.MESH
EPS = 1e-05
ROOT_HALF = 0.7071067811865476
INV_ROOT_TAU = 0.3989422804014327

WIDTH = (768, 256, 1024, 1024)
BASE = (0, 768, 1024, 2048)
PIECES = (
    ((0, 0, 256), (1, 256, 256), (2, 512, 256)),
    ((0, 0, 128), (2, 128, 128)),
    ((0, 0, 384), (1, 384, 384), (2, 768, 256)),
    ((0, 0, 256), (1, 256, 384), (2, 640, 384)),
)
ORDER = (("x", "z", "y"), ("z", "y", "x"), ("y", "x", "z"))
PIECE_LIST = [(g, i) for g in range(4) for i in range(len(PIECES[g]))]
SLOT = {(g, i): n for n, (g, i) in enumerate(PIECE_LIST)}
NP = len(PIECE_LIST)


def block_dims(axes_all):
    return (
        2 if "y" in axes_all else 1,
        4 if "x" in axes_all else 1,
        4 if "z" in axes_all else 1,
        2 if "y" in axes_all else 1,
    )


def dot(a, b, ca, cb):
    return lax.dot_general(a, b, (((ca,), (cb,)), ((), ())), preferred_element_type=F32)


def kernel(*refs):
    refs = list(refs)

    def take(n):
        out = refs[:n]
        del refs[:n]
        return out

    pw, tok, cot, vec = take(4)
    enc_out, gtok_out, gw_out, small_out = take(4)
    W = take(4)
    G = [None] * 4
    (G[3],) = take(1)
    G[2], G[1], G[0] = W[3], W[1], W[2]
    (X, C, Q, K, V, PR, MX, N1, INV1, H, ACT, SL, GR, GD, GM, ENC, GTR) = take(17)
    DQ, DK, DV, GTS = Q, K, V, H.at[pl.ds(0, 256)]
    S, R1, R2, R3, R4 = take(5)
    ACC, SVA, SVB, EXA, EXB, FIN = take(6)
    rs1 = take(NP * 3)
    rs2 = take(NP * 3)
    (ag_send, ag_recv, rs_send, rs_recv, ex_send, ex_recv, io_send, io_recv, io_loc) = take(9)
    (sm_send, sm_recv, smx_send, smx_recv, pw_send, pw_recv, fin_send, fin_recv) = take(8)

    dp = lax.axis_index("dp")
    th = lax.axis_index("tensor")
    c = dp % 2
    yl = (dp // 2) % 2
    z = (dp // 4) % 4
    x = dp // 16
    y = th * 2 + yl
    me = {"x": x, "y": y, "z": z}

    def device(xx, yy, zz, cc):
        return (((xx * 4 + zz) * 2 + yy % 2) * 2 + cc, yy // 2)

    def nbr(axis, d):
        xx, yy, zz = x, y, z
        if axis == "x":
            xx = (x + d) % 4
        if axis == "y":
            yy = (y + d) % 4
        if axis == "z":
            zz = (z + d) % 4
        return device(xx, yy, zz, c)

    mate = device(x, y, z, 1 - c)
    partner = (((x * 4 + z) * 2 + yl) * 2 + (1 - c), 1 - th)
    stays = c == th

    def remote(src, dst, ss, rs, to):
        return pltpu.make_async_remote_copy(
            src_ref=src, dst_ref=dst, send_sem=ss, recv_sem=rs, device_id=to, device_id_type=MESH
        )

    barrier = pltpu.get_barrier_semaphore()
    talk = [nbr(a, d) for a in ("x", "y", "z") for d in (1, 2, 3)] + [mate, partner]
    for to in talk:
        pl.semaphore_signal(barrier, inc=1, device_id=to, device_id_type=MESH)
    pl.semaphore_wait(barrier, len(talk))

    def chip_rows(core):
        return pl.ds(pl.multiple_of(core * 16, 16), 16)

    def own_slot(ref, rows, cols):
        return ref.at[th, x, z, yl, rows, cols]

    def pw_copy(g):
        cols = pl.ds(BASE[g], WIDTH[g])
        return remote(
            pw.at[1 - c, :, cols],
            own_slot(W[g], chip_rows(c), pl.ds(0, WIDTH[g])),
            pw_send.at[g],
            pw_recv.at[g],
            mate,
        )

    for g in range(4):
        pw_copy(g).start()

    own_half = pl.ds(pl.multiple_of(c * 256, 256), 256)

    def swap_in(src, buf, i):
        to_partner = remote(
            src, buf.at[pl.ds(pl.multiple_of(th * 256, 256), 256)], io_send.at[i], io_recv.at[i], partner
        )
        local = pltpu.make_async_copy(src, buf.at[own_half], io_loc.at[i])
        return to_partner, local

    def to_mate(buf, i):
        return remote(buf.at[own_half], buf.at[own_half], io_send.at[2 + i], io_recv.at[2 + i], mate)

    swaps = [swap_in(tok, X, 0), swap_in(cot, C, 1)]

    @pl.when(stays)
    def _():
        for a, b in swaps:
            b.start()

    @pl.when(jnp.logical_not(stays))
    def _():
        swaps[0][0].start()

    for g in range(4):
        W[g][th, x, z, yl, chip_rows(c), :] = pw[c, :, BASE[g] : BASE[g] + WIDTH[g]]

    def ag_block(g, i, p, coords, rows):
        colour, off, n = PIECES[g][i]
        order = ORDER[colour]
        known = order[:p]
        sel = []
        for axis in ("x", "z"):
            sel.append(pl.ds(0, 4) if axis in known else pl.ds(coords[axis], 1))
        if "y" in known:
            hs, ys = pl.ds(0, 2), pl.ds(0, 2)
        else:
            hs, ys = pl.ds(coords["y"] // 2, 1), pl.ds(coords["y"] % 2, 1)
        return W[g].at[hs, sel[0], sel[1], ys, rows, pl.ds(off, n)]

    def ag_copy(g, i, p, which):
        s = SLOT[g, i]
        axis = ORDER[PIECES[g][i][0]][p]
        at = me[axis]
        if which < 2:
            ref = ag_block(g, i, p, me, pl.ds(0, 32))
            to = nbr(axis, 1 if which == 0 else 3)
        elif which == 2:
            ref = ag_block(g, i, p, {**me, axis: (at + 3) % 4}, pl.ds(0, 16))
            to = nbr(axis, 1)
        else:
            ref = ag_block(g, i, p, {**me, axis: (at + 1) % 4}, pl.ds(16, 16))
            to = nbr(axis, 3)
        return remote(ref, ref, ag_send.at[s, p, which], ag_recv.at[s, p, which], to)

    def ag_step(g, step):
        if step == 0:
            pw_copy(g).wait()
        p, sub = divmod(step, 2)
        for i in range(len(PIECES[g])):
            if sub == 0:
                if p > 0:
                    ag_copy(g, i, p - 1, 2).wait_recv()
                    ag_copy(g, i, p - 1, 3).wait_recv()
                if p < 3:
                    ag_copy(g, i, p, 0).start()
                    ag_copy(g, i, p, 1).start()
            else:
                ag_copy(g, i, p, 0).wait_recv()
                ag_copy(g, i, p, 2).start()
                ag_copy(g, i, p, 1).wait_recv()
                ag_copy(g, i, p, 3).start()

    def ag_drain(g):
        for i in range(len(PIECES[g])):
            for p in range(3):
                for which in range(4):
                    ag_copy(g, i, p, which).wait_send()

    def wave(t):
        for g in range(4):
            if 0 <= t - g <= 6:
                ag_step(g, t - g)

    wave(0)
    wave(1)

    @pl.when(stays)
    def _():
        swaps[0][1].wait()
        swaps[1][1].wait()

    @pl.when(jnp.logical_not(stays))
    def _():
        swaps[0][0].wait()
        swaps[1][0].start()

    to_mate(X, 0).start()
    for t in range(2, 7):
        wave(t)
    to_mate(X, 0).wait()

    qkv_dst = (Q, K, V)
    lanes = lax.broadcasted_iota(jnp.int32, (1, 128), 1)

    def project(j, hh):
        w = W[0][hh, :, :, :, :, j * 256 : (j + 1) * 256].reshape(1024, 256)
        out = dot(X[...], w, 1, 0)
        if j != 1:
            row = 0 if j == 0 else 1
            start = pl.multiple_of(hh * 512 + c * 256, 256)
            out = out + vec[row : row + 1, pl.ds(start, 256)]
        out = out.astype(BF16)
        if j == 0:
            out = out * jnp.asarray(0.125, BF16)
        qkv_dst[j][:, pl.ds(pl.multiple_of(hh * 256, 256), 256)] = out

    def project_all(hh, carry):
        for j in range(3):
            project(j, hh)
        return carry

    lax.fori_loop(0, 2, project_all, 0)

    wave(7)

    def head_mask(j):
        return (lanes < 64) if j == 0 else (lanes >= 64)

    def only(v, j):
        return jnp.where(head_mask(j), v, jnp.zeros_like(v))

    def attend(p, carry):
        cols = pl.ds(pl.multiple_of(p * 128, 128), 128)
        k2 = K[:, cols]
        v2 = V[:, cols]
        for r in range(2):
            rows = slice(r * 256, (r + 1) * 256)
            q2 = Q[rows, cols]
            acc = None
            for j in range(2):
                s = dot(only(q2, j), k2, 1, 1)
                s = jnp.exp(s - jnp.max(s, axis=-1, keepdims=True))
                s = s * (1.0 / jnp.sum(s, axis=-1, keepdims=True))
                pr = s.astype(BF16)
                PR[p * 2 + j, rows, :] = pr
                o = dot(pr, only(v2, j), 1, 0)
                acc = o if acc is None else acc + o
            MX[rows, cols] = acc.astype(BF16)
        return carry

    lax.fori_loop(0, 4, attend, 0)
    wave(8)

    def ex_copy(e, dst, i):
        cols = pl.ds(pl.multiple_of(i * 256, 256), 256)
        return remote(S.at[:, cols], dst.at[:, cols], ex_send.at[e, i], ex_recv.at[e, i], mate)

    def out_part(i, carry):
        acc = None
        for hh in range(2):
            w = W[1][hh, i].reshape(256, 256)
            o = dot(MX[:, hh * 256 : (hh + 1) * 256], w, 1, 1)
            acc = o if acc is None else acc + o
        S[:, pl.ds(pl.multiple_of(i * 256, 256), 256)] = acc.astype(BF16)
        ex_copy(0, R1, i).start()
        return carry

    lax.fori_loop(0, 4, out_part, 0)
    wave(9)

    def ex_wait(e, dst):
        for i in range(4):
            ex_copy(e, dst, i).wait()

    ex_wait(0, R1)

    def mean(v):
        return jnp.sum(v, axis=-1, keepdims=True) * (1.0 / 1024)

    def ln1(i, carry):
        rows = pl.ds(pl.multiple_of(i * 32, 32), 32)
        r = X[rows].astype(F32) + (S[rows].astype(F32) + R1[rows].astype(F32)) + vec[2:3]
        cen = r - mean(r)
        inv = lax.rsqrt(mean(cen * cen) + EPS)
        n = cen * inv
        N1[rows] = n
        INV1[rows] = jnp.broadcast_to(inv, (32, 128))
        H[rows] = (n * vec[3:4] + vec[4:5]).astype(BF16)
        return carry

    lax.fori_loop(0, 16, ln1, 0)

    def up(i, carry):
        cols = pl.ds(pl.multiple_of(i * 256, 256), 256)
        for hh in range(2):
            w = W[2][hh, :, :, :, :, cols].reshape(1024, 256)
            u = dot(H[...], w, 1, 0)
            u = u + vec[pl.ds(5 + hh * 2 + c, 1), cols]
            e = 0.5 * (1.0 + lax.erf(u * ROOT_HALF))
            dst = pl.ds(pl.multiple_of(hh * 1024 + i * 256, 256), 256)
            ACT[:, dst] = (u * e).astype(BF16)
            SL[:, dst] = (e + u * jnp.exp(-0.5 * u * u) * INV_ROOT_TAU).astype(BF16)
        return carry

    lax.fori_loop(0, 4, up, 0)

    def down(i, carry):
        acc = None
        for hh in range(2):
            w = W[3][hh, i].reshape(256, 1024)
            o = dot(ACT[:, hh * 1024 : (hh + 1) * 1024], w, 1, 1)
            acc = o if acc is None else acc + o
        S[:, pl.ds(pl.multiple_of(i * 256, 256), 256)] = acc.astype(BF16)
        ex_copy(1, R2, i).start()
        return carry

    lax.fori_loop(0, 4, down, 0)

    @pl.when(jnp.logical_not(stays))
    def _():
        swaps[1][0].wait()

    to_mate(C, 1).start()
    for g in range(4):
        ag_drain(g)
    to_mate(C, 1).wait()
    ex_wait(1, R2)

    ACC[...] = jnp.zeros_like(ACC)

    def fold(v):
        return v[0:8] + v[8:16] + (v[16:24] + v[24:32])

    def ln2(i, carry):
        rows = pl.ds(pl.multiple_of(i * 32, 32), 32)
        hidden = N1[rows] * vec[3:4] + vec[4:5]
        r = hidden + (S[rows].astype(F32) + R2[rows].astype(F32)) + vec[9:10]
        cen = r - mean(r)
        inv = lax.rsqrt(mean(cen * cen) + EPS)
        n = cen * inv
        ENC[rows] = (n * vec[10:11] + vec[11:12]).astype(BF16)
        g = C[rows].astype(F32)
        ACC[1] += fold(g * n)
        ACC[2] += fold(g)
        sc = g * vec[10:11]
        gr = inv * (sc - mean(sc) - n * mean(sc * n))
        ACC[0] += fold(gr)
        GR[rows] = gr
        GD[rows] = gr.astype(BF16)
        return carry

    lax.fori_loop(0, 16, ln2, 0)

    enc_local = pltpu.make_async_copy(ENC.at[own_half], enc_out, io_loc.at[2])
    enc_remote = remote(ENC.at[own_half], enc_out, io_send.at[4], io_recv.at[4], partner)

    def rs_axis(g, i, p):
        return ORDER[PIECES[g][i][0]][2 - p]

    def rs_open(g, i, p):
        return ORDER[PIECES[g][i][0]][: 2 - p]

    def rs_base(g, i, p, coord):
        opened = rs_open(g, i, p)
        at = {**me, rs_axis(g, i, p): coord}
        zero = jnp.int32(0)
        base = (
            zero if "y" in opened else at["y"] // 2,
            zero if "x" in opened else at["x"],
            zero if "z" in opened else at["z"],
            zero if "y" in opened else at["y"] % 2,
        )
        return base, block_dims(opened)

    def rs_block(g, i, p, coord, rows):
        base, dims = rs_base(g, i, p, coord)
        _, off, n = PIECES[g][i]
        return G[g].at[
            pl.ds(base[0], dims[0]),
            pl.ds(base[1], dims[1]),
            pl.ds(base[2], dims[2]),
            pl.ds(base[3], dims[3]),
            rows,
            pl.ds(off, n),
        ]

    def rs_copy(g, i, p, which):
        s = SLOT[g, i]
        axis = rs_axis(g, i, p)
        at = me[axis]
        far = (at + 2) % 4
        lower, upper = (at + 3) % 4, (at + 1) % 4
        if which == 0:
            src, dst, to = rs_block(g, i, p, far, pl.ds(0, 16)), rs1[s * 3 + p].at[0], nbr(axis, 3)
        elif which == 1:
            src, dst, to = rs_block(g, i, p, far, pl.ds(16, 16)), rs1[s * 3 + p].at[1], nbr(axis, 1)
        elif which == 2:
            src, dst, to = rs_block(g, i, p, lower, pl.ds(0, 32)), rs2[s * 3 + p].at[0], nbr(axis, 3)
        else:
            src, dst, to = rs_block(g, i, p, upper, pl.ds(0, 32)), rs2[s * 3 + p].at[1], nbr(axis, 1)
        return remote(src, dst, rs_send.at[s, p, which], rs_recv.at[s, p, which], to)

    def unflatten(i, dims):
        out = []
        for d in reversed(dims):
            out.append(i % d if d > 1 else 0)
            i = i // d if d > 1 else i
        return tuple(reversed(out))

    def rs_mid(g, i, p, which):
        s = SLOT[g, i]
        _, off, n = PIECES[g][i]
        at = me[rs_axis(g, i, p)]
        coord = (at + 3) % 4 if which == 0 else (at + 1) % 4
        base, dims = rs_base(g, i, p, coord)
        rows = slice(which * 16, which * 16 + 16)
        buf = rs1[s * 3 + p]

        def one(k, carry):
            a = unflatten(k, dims)
            b = tuple(u + w for u, w in zip(base, a))
            total = G[g][(*b, rows, slice(off, off + n))].astype(F32) + buf[(which, *a)].astype(F32)
            G[g][(*b, rows, slice(off, off + n))] = total.astype(BF16)
            return carry

        lax.fori_loop(0, dims[0] * dims[1] * dims[2] * dims[3], one, 0)

    def rs_fin(g, i, p):
        s = SLOT[g, i]
        _, off, n = PIECES[g][i]
        base, dims = rs_base(g, i, p, me[rs_axis(g, i, p)])
        buf = rs2[s * 3 + p]

        def one(k, carry):
            a = unflatten(k, dims)
            b = tuple(u + w for u, w in zip(base, a))
            total = (
                G[g][(*b, slice(0, 32), slice(off, off + n))].astype(F32)
                + buf[(0, *a)].astype(F32)
                + buf[(1, *a)].astype(F32)
            )
            if p == 2:
                FIN[:, BASE[g] + off : BASE[g] + off + n] = total
            else:
                G[g][(*b, slice(0, 32), slice(off, off + n))] = total.astype(BF16)
            return carry

        if p == 2:
            one(0, 0)
        else:
            lax.fori_loop(0, dims[0] * dims[1] * dims[2] * dims[3], one, 0)

    def fin_copy(g):
        cols = pl.ds(BASE[g], WIDTH[g])
        return remote(
            FIN.at[chip_rows(1 - c), cols],
            gw_out.at[c, :, cols],
            fin_send.at[g],
            fin_recv.at[g],
            mate,
        )

    def rs_step(g, step):
        p, sub = divmod(step, 2)
        for i in range(len(PIECES[g])):
            if sub == 0:
                if p > 0:
                    rs_copy(g, i, p - 1, 2).wait()
                    rs_copy(g, i, p - 1, 3).wait()
                    rs_fin(g, i, p - 1)
                if p < 3:
                    rs_copy(g, i, p, 0).start()
                    rs_copy(g, i, p, 1).start()
            else:
                rs_copy(g, i, p, 0).wait()
                rs_mid(g, i, p, 0)
                rs_copy(g, i, p, 2).start()
                rs_copy(g, i, p, 1).wait()
                rs_mid(g, i, p, 1)
                rs_copy(g, i, p, 3).start()
        if step == 6:
            cols = slice(BASE[g], BASE[g] + WIDTH[g])
            gw_out[pl.ds(c, 1), :, cols] = FIN[chip_rows(c), cols].reshape(1, 16, WIDTH[g])
            fin_copy(g).start()

    def weight_grad(g, a_ref, sources):
        def one(i, carry):
            a = a_ref[:, pl.ds(pl.multiple_of(i * 256, 256), 256)]
            for hh in range(2):
                at = 0
                for ref, starts, n in sources:
                    o = dot(a, ref[:, starts[hh] : starts[hh] + n], 0, 0)
                    G[g][hh, i, :, :, :, at : at + n] = o.astype(BF16).reshape(4, 2, 32, n)
                    at += n
            return carry

        lax.fori_loop(0, 4, one, 0)

    weight_grad(3, GD, [(ACT, (0, 1024), 1024)])
    rs_step(3, 0)

    @pl.when(stays)
    def _():
        enc_local.start()

    @pl.when(jnp.logical_not(stays))
    def _():
        enc_remote.start()

    def grad_up(i, carry):
        cols = pl.ds(pl.multiple_of(i * 256, 256), 256)
        for hh in range(2):
            w = W[3][hh, :, :, :, :, cols].reshape(1024, 256)
            dst = pl.ds(pl.multiple_of(hh * 1024 + i * 256, 256), 256)
            gu = (dot(GD[...], w, 1, 0) * SL[:, dst].astype(F32)).astype(BF16)
            SL[:, dst] = gu
            SVA[0, pl.ds(x, 1), hh : hh + 1, cols] = jnp.sum(
                gu.astype(F32), axis=0, keepdims=True
            ).reshape(1, 1, 256)
        return carry

    lax.fori_loop(0, 4, grad_up, 0)

    def hidden_part(i, carry):
        acc = None
        for hh in range(2):
            w = W[2][hh, i].reshape(256, 1024)
            o = dot(SL[:, hh * 1024 : (hh + 1) * 1024], w, 1, 1)
            acc = o if acc is None else acc + o
        S[:, pl.ds(pl.multiple_of(i * 256, 256), 256)] = acc.astype(BF16)
        ex_copy(2, R3, i).start()
        return carry

    lax.fori_loop(0, 4, hidden_part, 0)
    weight_grad(2, H, [(SL, (0, 1024), 1024)])
    rs_step(2, 0)
    rs_step(3, 1)
    ex_wait(2, R3)

    def ln1_back(i, carry):
        rows = pl.ds(pl.multiple_of(i * 32, 32), 32)
        gh = GR[rows] + (S[rows].astype(F32) + R3[rows].astype(F32))
        n = N1[rows]
        ACC[3] += fold(gh * n)
        ACC[4] += fold(gh)
        sc = gh * vec[3:4]
        inv = INV1[rows][:, 0:1]
        gr = inv * (sc - mean(sc) - n * mean(sc * n))
        ACC[5] += fold(gr)
        GR[rows] = gr
        GD[rows] = gr.astype(BF16)
        return carry

    lax.fori_loop(0, 16, ln1_back, 0)
    for i in range(6):
        SVA[0, pl.ds(x, 1), 2 + i : 3 + i, :] = jnp.sum(ACC[i], axis=0, keepdims=True).reshape(1, 1, 1024)

    SM_AXES = ("x", "z", "y")

    def sm_copy(buf, b, p, d):
        axis = SM_AXES[p]
        ref = buf.at[p, me[axis]]
        return remote(ref, ref, sm_send.at[b, p, d - 1], sm_recv.at[b, p, d - 1], nbr(axis, d))

    def sm_start(buf, b, p):
        for d in (1, 2, 3):
            sm_copy(buf, b, p, d).start()

    def sm_fin(buf, b, p, last):
        for d in (1, 2, 3):
            sm_copy(buf, b, p, d).wait()
        total = (buf[p, 0] + buf[p, 1]) + (buf[p, 2] + buf[p, 3])
        if p < 2:
            buf[p + 1, pl.ds(me[SM_AXES[p + 1]], 1)] = total.reshape(1, *total.shape)
        else:
            last[0] = total

    def smx_copy(ex, b):
        return remote(ex.at[0], ex.at[1], smx_send.at[b], smx_recv.at[b], mate)

    sm_start(SVA, 0, 0)

    for hh in range(2):
        w = W[1][hh].reshape(1024, 256)
        GM[:, hh * 256 : (hh + 1) * 256] = dot(GD[...], w, 1, 0).astype(BF16)
    weight_grad(1, GD, [(MX, (0, 256), 256)])
    rs_step(1, 0)
    rs_step(3, 2)

    def attend_back(p, carry):
        cols = pl.ds(pl.multiple_of(p * 128, 128), 128)
        q2 = Q[:, cols]
        k2 = K[:, cols]
        v2 = V[:, cols]
        gm2 = GM[:, cols]
        dk = None
        dq = None
        dv = None
        for j in range(2):
            gmj = only(gm2, j)
            pr = PR[p * 2 + j]
            prf = pr.astype(F32)
            gp = dot(gmj, v2, 1, 1)
            row = jnp.sum(prf * gp, axis=-1, keepdims=True)
            ds = (prf * (gp - row)).astype(BF16)
            a = dot(ds, only(k2, j), 1, 0)
            b = dot(ds, only(q2, j), 0, 0)
            e = dot(pr, gmj, 0, 0)
            dq = a if dq is None else dq + a
            dk = b if dk is None else dk + b
            dv = e if dv is None else dv + e
        dq = (dq * 0.125).astype(BF16)
        dv = dv.astype(BF16)
        DQ[:, cols] = dq
        DK[:, cols] = dk.astype(BF16)
        DV[:, cols] = dv
        SVB[0, pl.ds(x, 1), pl.ds(p, 1), :] = jnp.sum(dq.astype(F32), axis=0, keepdims=True).reshape(1, 1, 128)
        SVB[0, pl.ds(x, 1), pl.ds(4 + p, 1), :] = jnp.sum(dv.astype(F32), axis=0, keepdims=True).reshape(1, 1, 128)
        return carry

    lax.fori_loop(0, 2, attend_back, 0)
    rs_step(2, 1)
    rs_step(3, 3)
    sm_fin(SVA, 0, 0, EXA)
    sm_start(SVA, 0, 1)
    lax.fori_loop(2, 4, attend_back, 0)

    weight_grad(0, X, [(DQ, (0, 256), 256), (DK, (0, 256), 256), (DV, (0, 256), 256)])
    rs_step(0, 0)
    sm_start(SVB, 1, 0)
    rs_step(1, 1)
    rs_step(2, 2)
    rs_step(3, 4)
    sm_fin(SVA, 0, 1, EXA)
    sm_start(SVA, 0, 2)

    other_half = pl.ds(pl.multiple_of((1 - c) * 256, 256), 256)

    def rows_part(i, carry):
        cols = pl.ds(pl.multiple_of(i * 256, 256), 256)
        acc = None
        for hh in range(2):
            for j, ref in enumerate((DQ, DK, DV)):
                w = W[0][hh, i, :, :, :, j * 256 : (j + 1) * 256].reshape(256, 256)
                o = dot(ref[:, hh * 256 : (hh + 1) * 256], w, 1, 1)
                acc = o if acc is None else acc + o
        S[:, cols] = acc.astype(BF16)
        return carry

    lax.fori_loop(0, 4, rows_part, 0)
    rows_copy = remote(S.at[other_half], R4, ex_send.at[3, 0], ex_recv.at[3, 0], mate)
    rows_copy.start()
    rows_copy.wait()

    def finish(i, carry):
        here = pl.ds(pl.multiple_of(c * 256 + i * 32, 32), 32)
        rows = pl.ds(pl.multiple_of(i * 32, 32), 32)
        total = GR[here] + (S[here].astype(F32) + R4[rows].astype(F32))
        gtok_out[rows] = total
        GTS[rows] = total.astype(BF16)
        return carry

    lax.fori_loop(0, 8, finish, 0)
    gt_remote = remote(GTS, GTR, io_send.at[5], io_recv.at[5], partner)

    @pl.when(jnp.logical_not(stays))
    def _():
        gt_remote.start()

    rs_step(0, 1)
    sm_fin(SVB, 1, 0, EXB)
    sm_start(SVB, 1, 1)
    rs_step(1, 2)
    rs_step(2, 3)
    rs_step(3, 5)
    sm_fin(SVA, 0, 2, EXA)
    smx_copy(EXA, 0).start()
    rs_step(0, 2)
    sm_fin(SVB, 1, 1, EXB)
    sm_start(SVB, 1, 2)
    rs_step(1, 3)
    rs_step(2, 4)
    rs_step(3, 6)
    rs_step(0, 3)
    rs_step(1, 4)
    rs_step(2, 5)
    sm_fin(SVB, 1, 2, EXB)
    smx_copy(EXB, 1).start()
    rs_step(0, 4)
    rs_step(1, 5)
    rs_step(2, 6)
    rs_step(0, 5)
    rs_step(1, 6)
    smx_copy(EXA, 0).wait()
    smx_copy(EXB, 1).wait()
    small_out[...] = jnp.zeros_like(small_out)
    first = c == 0
    own_a, oth_a = EXA[0], EXA[1]
    low_a = jnp.where(first, own_a, oth_a)
    high_a = jnp.where(first, oth_a, own_a)
    for hh in range(2):
        small_out[5 + 2 * hh : 6 + 2 * hh, :] = low_a[hh : hh + 1]
        small_out[6 + 2 * hh : 7 + 2 * hh, :] = high_a[hh : hh + 1]
    for src, dst in ((2, 9), (3, 10), (4, 11), (5, 3), (6, 4), (7, 2)):
        small_out[dst : dst + 1, :] = low_a[src : src + 1]
    own_b, oth_b = EXB[0], EXB[1]
    parts_b = (jnp.where(first, own_b, oth_b), jnp.where(first, oth_b, own_b))
    for j in range(2):
        for hh in range(2):
            for cc in range(2):
                for u in range(2):
                    col = hh * 512 + cc * 256 + u * 128
                    k = j * 4 + hh * 2 + u
                    small_out[j : j + 1, col : col + 128] = parts_b[cc][k : k + 1]
    rs_step(0, 6)

    @pl.when(stays)
    def _():
        enc_local.wait()

    @pl.when(jnp.logical_not(stays))
    def _():
        enc_remote.wait()
        gt_remote.wait()

        def widen(i, carry):
            rows = pl.ds(pl.multiple_of(i * 32, 32), 32)
            gtok_out[rows] = GTR[rows].astype(F32)
            return carry

        lax.fori_loop(0, 8, widen, 0)

    for g in range(4):
        fin_copy(g).wait()


def scratch_list():
    def vm(shape, dtype=BF16):
        return pltpu.VMEM(shape, dtype)

    def weights(n):
        return vm((2, 4, 4, 2, 32, n))

    out = [weights(n) for n in WIDTH] + [weights(1024)]
    out += [vm((512, 1024)), vm((512, 1024))]
    out += [vm((512, 512))] * 3
    out += [vm((8, 512, 512)), vm((512, 512))]
    out += [vm((512, 1024), F32), vm((512, 128), F32), vm((512, 1024))]
    out += [vm((512, 2048)), vm((512, 2048))]
    out += [vm((512, 1024), F32), vm((512, 1024))]
    out += [vm((512, 512)), vm((512, 1024)), vm((256, 1024))]
    out += [vm((512, 1024))] * 4 + [vm((256, 1024))]
    out += [vm((6, 8, 1024), F32), vm((3, 4, 8, 1024), F32), vm((3, 4, 8, 128), F32)]
    out += [vm((2, 8, 1024), F32), vm((2, 8, 128), F32), vm((32, 3072), F32)]
    for rows in (16, 32):
        for g, i in PIECE_LIST:
            colour, _, n = PIECES[g][i]
            for p in range(3):
                out.append(vm((2, *block_dims(ORDER[colour][: 2 - p]), rows, n)))
    dma = pltpu.SemaphoreType.DMA
    out += [dma((NP, 3, 4))] * 4
    out += [dma((4, 4)), dma((4, 4)), dma((6,)), dma((6,)), dma((3,))]
    out += [dma((2, 3, 3)), dma((2, 3, 3)), dma((2,)), dma((2,))]
    out += [dma((4,))] * 4
    return out


def body(
    tokens,
    w_qkv,
    b_qv,
    w_out,
    b_out,
    gain_attn,
    shift_attn,
    w_in,
    b_in,
    w_back,
    b_back,
    gain_ffn,
    shift_ffn,
    cotangent,
):
    def halves(m, n):
        return m.reshape(16, 2, n).transpose(1, 0, 2)

    qkv = w_qkv[0].reshape(16, 3, 2, 256).transpose(2, 0, 1, 3).reshape(2, 16, 768)
    packed = jnp.concatenate(
        [qkv, halves(w_out[0].T, 256), halves(w_in[0], 1024), halves(w_back[0].T, 1024)], axis=2
    )
    vec = jnp.concatenate(
        [
            b_qv.reshape(2, 1024),
            b_out,
            gain_attn,
            shift_attn,
            b_in.reshape(4, 1024),
            b_back,
            gain_ffn,
            shift_ffn,
            jnp.zeros((4, 1024), BF16),
        ],
        axis=0,
    ).astype(F32)
    vmem = pl.BlockSpec(memory_space=pltpu.VMEM)
    hbm = pl.BlockSpec(memory_space=pl.ANY)
    enc, gtok, gw, small = pl.pallas_call(
        kernel,
        out_shape=(
            jax.ShapeDtypeStruct((256, 1024), BF16),
            jax.ShapeDtypeStruct((256, 1024), F32),
            jax.ShapeDtypeStruct((2, 16, 3072), F32),
            jax.ShapeDtypeStruct((16, 1024), F32),
        ),
        in_specs=[vmem, hbm, hbm, vmem],
        out_specs=(hbm, vmem, vmem, vmem),
        scratch_shapes=scratch_list(),
        compiler_params=pltpu.CompilerParams(
            collective_id=0, has_side_effects=True, vmem_limit_bytes=60 * 1024 * 1024
        ),
        cost_estimate=pl.CostEstimate(
            flops=22_000_000_000, bytes_accessed=5_000_000, transcendentals=6_000_000
        ),
        name="encoder_layer",
    )(packed, tokens, cotangent, vec)

    def join(col, n):
        return gw[:, :, col : col + n].transpose(1, 0, 2).reshape(16, 2 * n)

    g_qkv = gw[:, :, :768].reshape(2, 16, 3, 256).transpose(1, 2, 0, 3).reshape(1, 16, 3, 512)
    return (
        enc,
        gtok,
        g_qkv,
        small[0:2].reshape(1, 2, 1024),
        join(768, 256).T[None],
        small[2:3],
        small[3:4],
        small[4:5],
        join(1024, 1024)[None],
        small[5:9].reshape(1, 4096),
        join(2048, 1024).T[None],
        small[9:10],
        small[10:11],
        small[11:12],
    )


def solution(mesh):
    in_specs = (
        P(("dp", "tensor"), None),
        P(None, "dp", None, "tensor"),
        P(),
        P(None, "tensor", "dp"),
        P(),
        P(),
        P(),
        P(None, "dp", "tensor"),
        P(),
        P(None, "tensor", "dp"),
        P(),
        P(),
        P(),
        P(("dp", "tensor"), None),
    )
    out_specs = (
        P(("dp", "tensor"), None),
        P(("dp", "tensor"), None),
        P(None, "dp", None, "tensor"),
        P(),
        P(None, "tensor", "dp"),
        P(),
        P(),
        P(),
        P(None, "dp", "tensor"),
        P(),
        P(None, "tensor", "dp"),
        P(),
        P(),
        P(),
    )
    return jax.shard_map(body, mesh=mesh, in_specs=in_specs, out_specs=out_specs, check_vma=False)
```

```python
import jax
import jax.numpy as jnp
from jax import lax
from jax.experimental import pallas as pl
from jax.experimental.pallas import tpu as pltpu
from jax.sharding import PartitionSpec as P

F32 = jnp.float32
BF16 = jnp.bfloat16
MESH = pl.DeviceIdType.MESH
EPS = 1e-05
ROOT_HALF = 0.7071067811865476
INV_ROOT_TAU = 0.3989422804014327

WIDTH = (768, 256, 1024, 1024)
BASE = (0, 768, 1024, 2048)
PIECES = (
    ((0, 0, 256), (1, 256, 256), (2, 512, 256)),
    ((1, 0, 128), (2, 128, 128)),
    ((0, 0, 256), (1, 256, 384), (2, 640, 384)),
    ((0, 0, 256), (1, 256, 384), (2, 640, 384)),
)
ORDER = (("x", "z", "y"), ("z", "y", "x"), ("y", "x", "z"))
PIECE_LIST = [(g, i) for g in range(4) for i in range(len(PIECES[g]))]
SLOT = {(g, i): n for n, (g, i) in enumerate(PIECE_LIST)}
NP = len(PIECE_LIST)


def block_dims(axes_all):
    return (
        2 if "y" in axes_all else 1,
        4 if "x" in axes_all else 1,
        4 if "z" in axes_all else 1,
        2 if "y" in axes_all else 1,
    )


def dot(a, b, ca, cb):
    return lax.dot_general(a, b, (((ca,), (cb,)), ((), ())), preferred_element_type=F32)


def kernel(*refs):
    refs = list(refs)

    def take(n):
        out = refs[:n]
        del refs[:n]
        return out

    tok, cot, *raw = take(6)
    small_in = take(8)
    enc_out, gtok_out = take(2)
    gw_out = take(4)
    small_out = take(8)
    (vec,) = take(1)
    W = take(4)
    G = [None] * 4
    (G[3],) = take(1)
    G[2], G[1], G[0] = W[3], W[1], W[2]
    (X, C, Q, K, V, PR, MX, N1, INV1, H, ACT, SL, GR, GD, GM, ENC, GTR) = take(17)
    DQ, DK, DV, GTS = Q, K, V, H.at[pl.ds(0, 256)]
    S, R1, R2, R3, R4 = take(5)
    ACC, SVA, SVB, EXA, EXB, FIN = take(6)
    rs1 = take(NP)
    rs2 = take(NP * 3)
    (ag_send, ag_recv, rs_send, rs_recv, ex_send, ex_recv, io_send, io_recv, io_loc) = take(9)
    (sm_send, sm_recv, smx_send, smx_recv, pw_send, pw_recv, pw_loc, fin_send, fin_recv) = take(9)

    dp = lax.axis_index("dp")
    th = lax.axis_index("tensor")
    c = dp % 2
    yl = (dp // 2) % 2
    z = (dp // 4) % 4
    x = dp // 16
    y = th * 2 + yl
    me = {"x": x, "y": y, "z": z}

    def device(xx, yy, zz, cc):
        return (((xx * 4 + zz) * 2 + yy % 2) * 2 + cc, yy // 2)

    def nbr(axis, d):
        xx, yy, zz = x, y, z
        if axis == "x":
            xx = (x + d) % 4
        if axis == "y":
            yy = (y + d) % 4
        if axis == "z":
            zz = (z + d) % 4
        return device(xx, yy, zz, c)

    mate = device(x, y, z, 1 - c)
    partner = (((x * 4 + z) * 2 + yl) * 2 + (1 - c), 1 - th)
    stays = c == th

    def remote(src, dst, ss, rs, to):
        return pltpu.make_async_remote_copy(
            src_ref=src, dst_ref=dst, send_sem=ss, recv_sem=rs, device_id=to, device_id_type=MESH
        )

    barrier = pltpu.get_barrier_semaphore()
    talk = [nbr(a, d) for a in ("x", "y", "z") for d in (1, 2, 3)] + [mate, partner]
    for to in talk:
        pl.semaphore_signal(barrier, inc=1, device_id=to, device_id_type=MESH)
    pl.semaphore_wait(barrier, len(talk))

    def chip_rows(core):
        return pl.ds(pl.multiple_of(core * 16, 16), 16)

    def own_slot(ref, rows, cols):
        return ref.at[th, x, z, yl, rows, cols]

    RAW = [(0, j, j * 256, 256) for j in range(3)] + [(1, None, 0, 256), (2, None, 0, 1024), (3, None, 0, 1024)]

    def pw_pair(k):
        g, j, at, n = RAW[k]

        def src(t):
            cols = pl.ds(pl.multiple_of(t * n, n), n)
            return raw[g].at[j, :, cols] if g == 0 else raw[g].at[:, cols]

        dst = own_slot(W[g], chip_rows(c), pl.ds(at, n))
        away = remote(src(1 - c), dst, pw_send.at[k], pw_recv.at[k], mate)
        return away, pltpu.make_async_copy(src(c), dst, pw_loc.at[k])

    pairs = [pw_pair(k) for k in range(6)]
    for away, here in pairs:
        away.start()
        here.start()

    own_half = pl.ds(pl.multiple_of(c * 256, 256), 256)

    def swap_in(src, buf, i):
        to_partner = remote(
            src, buf.at[pl.ds(pl.multiple_of(th * 256, 256), 256)], io_send.at[i], io_recv.at[i], partner
        )
        local = pltpu.make_async_copy(src, buf.at[own_half], io_loc.at[i])
        return to_partner, local

    def to_mate(buf, i):
        return remote(buf.at[own_half], buf.at[own_half], io_send.at[2 + i], io_recv.at[2 + i], mate)

    swaps = [swap_in(tok, X, 0), swap_in(cot, C, 1)]

    @pl.when(stays)
    def _():
        for a, b in swaps:
            b.start()

    @pl.when(jnp.logical_not(stays))
    def _():
        swaps[0][0].start()

    def ag_block(g, i, p, coords, rows):
        colour, off, n = PIECES[g][i]
        order = ORDER[colour]
        known = order[:p]
        sel = []
        for axis in ("x", "z"):
            sel.append(pl.ds(0, 4) if axis in known else pl.ds(coords[axis], 1))
        if "y" in known:
            hs, ys = pl.ds(0, 2), pl.ds(0, 2)
        else:
            hs, ys = pl.ds(coords["y"] // 2, 1), pl.ds(coords["y"] % 2, 1)
        return W[g].at[hs, sel[0], sel[1], ys, rows, pl.ds(off, n)]

    def ag_copy(g, i, p, which):
        s = SLOT[g, i]
        axis = ORDER[PIECES[g][i][0]][p]
        at = me[axis]
        if which < 2 or p < 2:
            ref = ag_block(g, i, p, me, pl.ds(0, 32))
            to = nbr(axis, (1, 3, 2)[which])
        elif which == 2:
            ref = ag_block(g, i, p, {**me, axis: (at + 3) % 4}, pl.ds(0, 16))
            to = nbr(axis, 1)
        else:
            ref = ag_block(g, i, p, {**me, axis: (at + 1) % 4}, pl.ds(16, 16))
            to = nbr(axis, 3)
        return remote(ref, ref, ag_send.at[s, p, which], ag_recv.at[s, p, which], to)

    def ag_start(g, p):
        for i in range(len(PIECES[g])):
            for which in range(3 if p < 2 else 2):
                ag_copy(g, i, p, which).start()

    def ag_arrive(g, p):
        for i in range(len(PIECES[g])):
            for which in range(3):
                ag_copy(g, i, p, which).wait_recv()

    def ag_forward(g):
        for i in range(len(PIECES[g])):
            ag_copy(g, i, 2, 0).wait_recv()
            ag_copy(g, i, 2, 2).start()
            ag_copy(g, i, 2, 1).wait_recv()
            ag_copy(g, i, 2, 3).start()

    def ag_finish(g):
        for i in range(len(PIECES[g])):
            ag_copy(g, i, 2, 2).wait_recv()
            ag_copy(g, i, 2, 3).wait_recv()

    def ag_drain(g):
        for i in range(len(PIECES[g])):
            for p in range(3):
                for which in range(3 if p < 2 else 4):
                    ag_copy(g, i, p, which).wait_send()

    for g in range(4):
        for k in range(6):
            if RAW[k][0] == g:
                pairs[k][1].wait()
                pairs[k][0].wait()
        ag_start(g, 0)

    for i, ref in zip((0, 2, 3, 4, 5, 9, 10, 11), small_in):
        if i == 0:
            vec[0:2] = ref[0].astype(F32)
        elif i == 5:
            for k in range(4):
                vec[5 + k : 6 + k] = ref[:, k * 1024 : (k + 1) * 1024].astype(F32)
        else:
            vec[i : i + 1] = ref[...].astype(F32)

    for p in range(2):
        for g in range(4):
            ag_arrive(g, p)
            ag_start(g, p + 1)

    @pl.when(stays)
    def _():
        swaps[0][1].wait()
        swaps[1][1].wait()

    @pl.when(jnp.logical_not(stays))
    def _():
        swaps[0][0].wait()
        swaps[1][0].start()

    to_mate(X, 0).start()
    ag_forward(0)
    ag_forward(1)
    to_mate(X, 0).wait()
    ag_finish(0)

    qkv_dst = (Q, K, V)
    lanes = lax.broadcasted_iota(jnp.int32, (1, 128), 1)

    def project(j, hh):
        w = W[0][hh, :, :, :, :, j * 256 : (j + 1) * 256].reshape(1024, 256)
        out = dot(X[...], w, 1, 0)
        if j != 1:
            row = 0 if j == 0 else 1
            start = pl.multiple_of(hh * 512 + c * 256, 256)
            out = out + vec[row : row + 1, pl.ds(start, 256)]
        out = out.astype(BF16)
        if j == 0:
            out = out * jnp.asarray(0.125, BF16)
        qkv_dst[j][:, pl.ds(pl.multiple_of(hh * 256, 256), 256)] = out

    def project_all(hh, carry):
        for j in range(3):
            project(j, hh)
        return carry

    lax.fori_loop(0, 2, project_all, 0)
    ag_forward(2)

    def head_mask(j):
        return (lanes < 64) if j == 0 else (lanes >= 64)

    def only(v, j):
        return jnp.where(head_mask(j), v, jnp.zeros_like(v))

    def attend(p, carry):
        cols = pl.ds(pl.multiple_of(p * 128, 128), 128)
        k2 = K[:, cols]
        v2 = V[:, cols]
        for r in range(2):
            rows = slice(r * 256, (r + 1) * 256)
            q2 = Q[rows, cols]
            acc = None
            for j in range(2):
                s = dot(only(q2, j), k2, 1, 1)
                s = jnp.exp(s - jnp.max(s, axis=-1, keepdims=True))
                s = s * (1.0 / jnp.sum(s, axis=-1, keepdims=True))
                pr = s.astype(BF16)
                PR[p * 2 + j, rows, :] = pr
                o = dot(pr, only(v2, j), 1, 0)
                acc = o if acc is None else acc + o
            MX[rows, cols] = acc.astype(BF16)
        return carry

    lax.fori_loop(0, 4, attend, 0)
    ag_finish(1)

    def ex_copy(e, dst, i):
        cols = pl.ds(pl.multiple_of(i * 256, 256), 256)
        return remote(S.at[:, cols], dst.at[:, cols], ex_send.at[e, i], ex_recv.at[e, i], mate)

    def out_part(i, carry):
        acc = None
        for hh in range(2):
            w = W[1][hh, i].reshape(256, 256)
            o = dot(MX[:, hh * 256 : (hh + 1) * 256], w, 1, 1)
            acc = o if acc is None else acc + o
        S[:, pl.ds(pl.multiple_of(i * 256, 256), 256)] = acc.astype(BF16)
        ex_copy(0, R1, i).start()
        return carry

    lax.fori_loop(0, 4, out_part, 0)
    ag_forward(3)

    def ex_wait(e, dst):
        for i in range(4):
            ex_copy(e, dst, i).wait()

    ex_wait(0, R1)

    def mean(v):
        return jnp.sum(v, axis=-1, keepdims=True) * (1.0 / 1024)

    def ln1(i, carry):
        rows = pl.ds(pl.multiple_of(i * 32, 32), 32)
        r = X[rows].astype(F32) + (S[rows].astype(F32) + R1[rows].astype(F32)) + vec[2:3]
        cen = r - mean(r)
        inv = lax.rsqrt(mean(cen * cen) + EPS)
        n = cen * inv
        N1[rows] = n
        INV1[rows] = jnp.broadcast_to(inv, (32, 128))
        H[rows] = (n * vec[3:4] + vec[4:5]).astype(BF16)
        return carry

    lax.fori_loop(0, 16, ln1, 0, unroll=2)
    ag_finish(2)

    def up(i, carry):
        cols = pl.ds(pl.multiple_of(i * 256, 256), 256)
        for hh in range(2):
            w = W[2][hh, :, :, :, :, cols].reshape(1024, 256)
            u = dot(H[...], w, 1, 0)
            u = u + vec[pl.ds(5 + hh * 2 + c, 1), cols]
            e = 0.5 * (1.0 + lax.erf(u * ROOT_HALF))
            dst = pl.ds(pl.multiple_of(hh * 1024 + i * 256, 256), 256)
            ACT[:, dst] = (u * e).astype(BF16)
            SL[:, dst] = (e + u * jnp.exp(-0.5 * u * u) * INV_ROOT_TAU).astype(BF16)
        return carry

    lax.fori_loop(0, 4, up, 0)

    @pl.when(jnp.logical_not(stays))
    def _():
        swaps[1][0].wait()

    to_mate(C, 1).start()
    ag_finish(3)

    def down(i, carry):
        acc = None
        for hh in range(2):
            w = W[3][hh, i].reshape(256, 1024)
            o = dot(ACT[:, hh * 1024 : (hh + 1) * 1024], w, 1, 1)
            acc = o if acc is None else acc + o
        S[:, pl.ds(pl.multiple_of(i * 256, 256), 256)] = acc.astype(BF16)
        ex_copy(1, R2, i).start()
        return carry

    lax.fori_loop(0, 4, down, 0)

    for g in range(4):
        ag_drain(g)
    to_mate(C, 1).wait()
    ex_wait(1, R2)

    ACC[...] = jnp.zeros_like(ACC)

    def fold(v):
        return v[0:8] + v[8:16] + (v[16:24] + v[24:32])

    def ln2(i, carry):
        rows = pl.ds(pl.multiple_of(i * 32, 32), 32)
        hidden = N1[rows] * vec[3:4] + vec[4:5]
        r = hidden + (S[rows].astype(F32) + R2[rows].astype(F32)) + vec[9:10]
        cen = r - mean(r)
        inv = lax.rsqrt(mean(cen * cen) + EPS)
        n = cen * inv
        ENC[rows] = (n * vec[10:11] + vec[11:12]).astype(BF16)
        g = C[rows].astype(F32)
        ACC[1] += fold(g * n)
        ACC[2] += fold(g)
        sc = g * vec[10:11]
        gr = inv * (sc - mean(sc) - n * mean(sc * n))
        ACC[0] += fold(gr)
        GR[rows] = gr
        GD[rows] = gr.astype(BF16)
        return carry

    lax.fori_loop(0, 16, ln2, 0, unroll=2)

    enc_local = pltpu.make_async_copy(ENC.at[own_half], enc_out, io_loc.at[2])
    enc_remote = remote(ENC.at[own_half], enc_out, io_send.at[4], io_recv.at[4], partner)

    def rs_axis(g, i, p):
        return ORDER[PIECES[g][i][0]][2 - p]

    def rs_open(g, i, p):
        return ORDER[PIECES[g][i][0]][: 2 - p]

    def rs_base(g, i, p, coord):
        opened = rs_open(g, i, p)
        at = {**me, rs_axis(g, i, p): coord}
        zero = jnp.int32(0)
        base = (
            zero if "y" in opened else at["y"] // 2,
            zero if "x" in opened else at["x"],
            zero if "z" in opened else at["z"],
            zero if "y" in opened else at["y"] % 2,
        )
        return base, block_dims(opened)

    def rs_block(g, i, p, coord, rows):
        base, dims = rs_base(g, i, p, coord)
        _, off, n = PIECES[g][i]
        return G[g].at[
            pl.ds(base[0], dims[0]),
            pl.ds(base[1], dims[1]),
            pl.ds(base[2], dims[2]),
            pl.ds(base[3], dims[3]),
            rows,
            pl.ds(off, n),
        ]

    def rs_copy(g, i, p, which):
        s = SLOT[g, i]
        axis = rs_axis(g, i, p)
        at = me[axis]
        far = (at + 2) % 4
        lower, upper = (at + 3) % 4, (at + 1) % 4
        if p == 0 and which == 0:
            src, dst, to = rs_block(g, i, p, far, pl.ds(0, 16)), rs1[s].at[0], nbr(axis, 3)
        elif p == 0 and which == 1:
            src, dst, to = rs_block(g, i, p, far, pl.ds(16, 16)), rs1[s].at[1], nbr(axis, 1)
        elif which == 2:
            src, dst, to = rs_block(g, i, p, lower, pl.ds(0, 32)), rs2[s * 3 + p].at[0], nbr(axis, 3)
        elif which == 3:
            src, dst, to = rs_block(g, i, p, upper, pl.ds(0, 32)), rs2[s * 3 + p].at[1], nbr(axis, 1)
        else:
            src, dst, to = rs_block(g, i, p, far, pl.ds(0, 32)), rs2[s * 3 + p].at[2], nbr(axis, 2)
        return remote(src, dst, rs_send.at[s, p, which], rs_recv.at[s, p, which], to)

    def unflatten(i, dims):
        out = []
        for d in reversed(dims):
            out.append(i % d if d > 1 else 0)
            i = i // d if d > 1 else i
        return tuple(reversed(out))

    def rs_mid(g, i, p, which):
        s = SLOT[g, i]
        _, off, n = PIECES[g][i]
        at = me[rs_axis(g, i, p)]
        coord = (at + 3) % 4 if which == 0 else (at + 1) % 4
        base, dims = rs_base(g, i, p, coord)
        rows = slice(which * 16, which * 16 + 16)
        buf = rs1[s]

        def one(k, carry):
            a = unflatten(k, dims)
            b = tuple(u + w for u, w in zip(base, a))
            total = G[g][(*b, rows, slice(off, off + n))].astype(F32) + buf[(which, *a)].astype(F32)
            G[g][(*b, rows, slice(off, off + n))] = total.astype(BF16)
            return carry

        lax.fori_loop(0, dims[0] * dims[1] * dims[2] * dims[3], one, 0)

    def rs_fin(g, i, p):
        s = SLOT[g, i]
        _, off, n = PIECES[g][i]
        base, dims = rs_base(g, i, p, me[rs_axis(g, i, p)])
        buf = rs2[s * 3 + p]

        def one(k, carry):
            a = unflatten(k, dims)
            b = tuple(u + w for u, w in zip(base, a))
            total = (
                G[g][(*b, slice(0, 32), slice(off, off + n))].astype(F32)
                + buf[(0, *a)].astype(F32)
                + buf[(1, *a)].astype(F32)
            )
            if p > 0:
                total = total + buf[(2, *a)].astype(F32)
            if p == 2:
                FIN[:, BASE[g] + off : BASE[g] + off + n] = total
            else:
                G[g][(*b, slice(0, 32), slice(off, off + n))] = total.astype(BF16)
            return carry

        if p == 2:
            one(0, 0)
        else:
            lax.fori_loop(0, dims[0] * dims[1] * dims[2] * dims[3], one, 0)

    def fin_pair(k):
        g, j, at, n = RAW[k]
        cols = pl.ds(pl.multiple_of(c * n, n), n)
        dst = gw_out[g].at[j, :, cols] if g == 0 else gw_out[g].at[:, cols]
        src = slice(BASE[g] + at, BASE[g] + at + n)

        def keep():
            mine = FIN[chip_rows(c), src]
            if g == 0:
                gw_out[g][j, :, cols] = mine
            else:
                gw_out[g][:, cols] = mine

        away = remote(
            FIN.at[chip_rows(1 - c), pl.ds(BASE[g] + at, n)], dst, fin_send.at[k], fin_recv.at[k], mate
        )
        return away, keep

    fins = [fin_pair(k) for k in range(6)]

    def rs_step(g, step):
        for i in range(len(PIECES[g])):
            if step == 0:
                rs_copy(g, i, 0, 0).start()
                rs_copy(g, i, 0, 1).start()
            elif step == 1:
                rs_copy(g, i, 0, 0).wait()
                rs_mid(g, i, 0, 0)
                rs_copy(g, i, 0, 2).start()
                rs_copy(g, i, 0, 1).wait()
                rs_mid(g, i, 0, 1)
                rs_copy(g, i, 0, 3).start()
            else:
                p = step - 2
                for which in (2, 3) if p == 0 else (2, 3, 4):
                    rs_copy(g, i, p, which).wait()
                rs_fin(g, i, p)
                if p < 2:
                    for which in (2, 3, 4):
                        rs_copy(g, i, p + 1, which).start()
        if step == 4:
            for k in range(6):
                if RAW[k][0] == g:
                    fins[k][0].start()
                    fins[k][1]()

    def weight_grad(g, a_ref, sources):
        def one(i, carry):
            a = a_ref[:, pl.ds(pl.multiple_of(i * 256, 256), 256)]
            for hh in range(2):
                at = 0
                for ref, starts, n in sources:
                    o = dot(a, ref[:, starts[hh] : starts[hh] + n], 0, 0)
                    G[g][hh, i, :, :, :, at : at + n] = o.astype(BF16).reshape(4, 2, 32, n)
                    at += n
            return carry

        lax.fori_loop(0, 4, one, 0)

    weight_grad(3, GD, [(ACT, (0, 1024), 1024)])
    rs_step(3, 0)

    @pl.when(stays)
    def _():
        enc_local.start()

    @pl.when(jnp.logical_not(stays))
    def _():
        enc_remote.start()

    def grad_up(i, carry):
        cols = pl.ds(pl.multiple_of(i * 256, 256), 256)
        for hh in range(2):
            w = W[3][hh, :, :, :, :, cols].reshape(1024, 256)
            dst = pl.ds(pl.multiple_of(hh * 1024 + i * 256, 256), 256)
            gu = (dot(GD[...], w, 1, 0) * SL[:, dst].astype(F32)).astype(BF16)
            SL[:, dst] = gu
            SVA[0, pl.ds(x, 1), hh : hh + 1, cols] = jnp.sum(
                gu.astype(F32), axis=0, keepdims=True
            ).reshape(1, 1, 256)
        return carry

    lax.fori_loop(0, 4, grad_up, 0)

    def hidden_part(i, carry):
        acc = None
        for hh in range(2):
            w = W[2][hh, i].reshape(256, 1024)
            o = dot(SL[:, hh * 1024 : (hh + 1) * 1024], w, 1, 1)
            acc = o if acc is None else acc + o
        S[:, pl.ds(pl.multiple_of(i * 256, 256), 256)] = acc.astype(BF16)
        ex_copy(2, R3, i).start()
        return carry

    lax.fori_loop(0, 4, hidden_part, 0)
    weight_grad(2, H, [(SL, (0, 1024), 1024)])
    rs_step(2, 0)
    rs_step(3, 1)
    ex_wait(2, R3)

    def ln1_back(i, carry):
        rows = pl.ds(pl.multiple_of(i * 32, 32), 32)
        gh = GR[rows] + (S[rows].astype(F32) + R3[rows].astype(F32))
        n = N1[rows]
        ACC[3] += fold(gh * n)
        ACC[4] += fold(gh)
        sc = gh * vec[3:4]
        inv = INV1[rows][:, 0:1]
        gr = inv * (sc - mean(sc) - n * mean(sc * n))
        ACC[5] += fold(gr)
        GR[rows] = gr
        GD[rows] = gr.astype(BF16)
        return carry

    lax.fori_loop(0, 16, ln1_back, 0, unroll=2)
    for i in range(6):
        SVA[0, pl.ds(x, 1), 2 + i : 3 + i, :] = jnp.sum(ACC[i], axis=0, keepdims=True).reshape(1, 1, 1024)

    SM_AXES = ("x", "z", "y")

    def sm_copy(buf, b, p, d):
        axis = SM_AXES[p]
        ref = buf.at[p, me[axis]]
        return remote(ref, ref, sm_send.at[b, p, d - 1], sm_recv.at[b, p, d - 1], nbr(axis, d))

    def sm_start(buf, b, p):
        for d in (1, 2, 3):
            sm_copy(buf, b, p, d).start()

    def sm_fin(buf, b, p, last):
        for d in (1, 2, 3):
            sm_copy(buf, b, p, d).wait()
        total = (buf[p, 0] + buf[p, 1]) + (buf[p, 2] + buf[p, 3])
        if p < 2:
            buf[p + 1, pl.ds(me[SM_AXES[p + 1]], 1)] = total.reshape(1, *total.shape)
        else:
            last[0] = total

    def smx_copy(ex, b):
        return remote(ex.at[0], ex.at[1], smx_send.at[b], smx_recv.at[b], mate)

    sm_start(SVA, 0, 0)

    for hh in range(2):
        w = W[1][hh].reshape(1024, 256)
        GM[:, hh * 256 : (hh + 1) * 256] = dot(GD[...], w, 1, 0).astype(BF16)
    weight_grad(1, GD, [(MX, (0, 256), 256)])
    rs_step(1, 0)

    def attend_back(p, carry):
        cols = pl.ds(pl.multiple_of(p * 128, 128), 128)
        q2 = Q[:, cols]
        k2 = K[:, cols]
        v2 = V[:, cols]
        gm2 = GM[:, cols]
        dk = None
        dq = None
        dv = None
        for j in range(2):
            gmj = only(gm2, j)
            pr = PR[p * 2 + j]
            prf = pr.astype(F32)
            gp = dot(gmj, v2, 1, 1)
            row = jnp.sum(prf * gp, axis=-1, keepdims=True)
            ds = (prf * (gp - row)).astype(BF16)
            a = dot(ds, only(k2, j), 1, 0)
            b = dot(ds, only(q2, j), 0, 0)
            e = dot(pr, gmj, 0, 0)
            dq = a if dq is None else dq + a
            dk = b if dk is None else dk + b
            dv = e if dv is None else dv + e
        dq = (dq * 0.125).astype(BF16)
        dv = dv.astype(BF16)
        DQ[:, cols] = dq
        DK[:, cols] = dk.astype(BF16)
        DV[:, cols] = dv
        SVB[0, pl.ds(x, 1), pl.ds(p, 1), :] = jnp.sum(dq.astype(F32), axis=0, keepdims=True).reshape(1, 1, 128)
        SVB[0, pl.ds(x, 1), pl.ds(4 + p, 1), :] = jnp.sum(dv.astype(F32), axis=0, keepdims=True).reshape(1, 1, 128)
        return carry

    lax.fori_loop(0, 2, attend_back, 0)
    rs_step(2, 1)
    sm_fin(SVA, 0, 0, EXA)
    sm_start(SVA, 0, 1)
    lax.fori_loop(2, 4, attend_back, 0)

    weight_grad(0, X, [(DQ, (0, 256), 256), (DK, (0, 256), 256), (DV, (0, 256), 256)])
    rs_step(0, 0)
    sm_start(SVB, 1, 0)

    other_half = pl.ds(pl.multiple_of((1 - c) * 256, 256), 256)

    def rows_part(i, carry):
        cols = pl.ds(pl.multiple_of(i * 256, 256), 256)
        acc = None
        for hh in range(2):
            for j, ref in enumerate((DQ, DK, DV)):
                w = W[0][hh, i, :, :, :, j * 256 : (j + 1) * 256].reshape(256, 256)
                o = dot(ref[:, hh * 256 : (hh + 1) * 256], w, 1, 1)
                acc = o if acc is None else acc + o
        S[:, cols] = acc.astype(BF16)
        return carry

    lax.fori_loop(0, 4, rows_part, 0)
    rows_copy = remote(S.at[other_half], R4, ex_send.at[3, 0], ex_recv.at[3, 0], mate)
    rows_copy.start()
    rs_step(1, 1)
    rs_step(3, 2)
    sm_fin(SVA, 0, 1, EXA)
    sm_start(SVA, 0, 2)
    rows_copy.wait()

    def finish(i, carry):
        here = pl.ds(pl.multiple_of(c * 256 + i * 32, 32), 32)
        rows = pl.ds(pl.multiple_of(i * 32, 32), 32)
        total = GR[here] + (S[here].astype(F32) + R4[rows].astype(F32))
        gtok_out[rows] = total
        GTS[rows] = total.astype(BF16)
        return carry

    lax.fori_loop(0, 8, finish, 0)
    gt_remote = remote(GTS, GTR, io_send.at[5], io_recv.at[5], partner)

    @pl.when(jnp.logical_not(stays))
    def _():
        gt_remote.start()

    rs_step(0, 1)
    sm_fin(SVB, 1, 0, EXB)
    sm_start(SVB, 1, 1)
    rs_step(2, 2)
    rs_step(1, 2)
    rs_step(3, 3)
    sm_fin(SVA, 0, 2, EXA)
    smx_copy(EXA, 0).start()
    rs_step(0, 2)
    sm_fin(SVB, 1, 1, EXB)
    sm_start(SVB, 1, 2)
    rs_step(2, 3)
    rs_step(1, 3)
    rs_step(3, 4)
    rs_step(0, 3)
    sm_fin(SVB, 1, 2, EXB)
    smx_copy(EXB, 1).start()
    rs_step(2, 4)
    rs_step(1, 4)
    smx_copy(EXA, 0).wait()
    smx_copy(EXB, 1).wait()
    o_bqv, o_bout, o_ga, o_sa, o_bin, o_bb, o_gf, o_sf = small_out
    first = c == 0
    own_a, oth_a = EXA[0], EXA[1]
    low_a = jnp.where(first, own_a, oth_a)
    high_a = jnp.where(first, oth_a, own_a)
    for hh in range(2):
        o_bin[:, hh * 2048 : hh * 2048 + 1024] = low_a[hh : hh + 1]
        o_bin[:, hh * 2048 + 1024 : hh * 2048 + 2048] = high_a[hh : hh + 1]
    for src, dst in ((2, o_bb), (3, o_gf), (4, o_sf), (5, o_ga), (6, o_sa), (7, o_bout)):
        dst[...] = low_a[src : src + 1]
    own_b, oth_b = EXB[0], EXB[1]
    parts_b = (jnp.where(first, own_b, oth_b), jnp.where(first, oth_b, own_b))
    for j in range(2):
        for hh in range(2):
            for cc in range(2):
                for u in range(2):
                    col = hh * 512 + cc * 256 + u * 128
                    k = j * 4 + hh * 2 + u
                    o_bqv[0, j : j + 1, col : col + 128] = parts_b[cc][k : k + 1]
    rs_step(0, 4)

    @pl.when(stays)
    def _():
        enc_local.wait()

    @pl.when(jnp.logical_not(stays))
    def _():
        enc_remote.wait()
        gt_remote.wait()

        def widen(i, carry):
            rows = pl.ds(pl.multiple_of(i * 32, 32), 32)
            gtok_out[rows] = GTR[rows].astype(F32)
            return carry

        lax.fori_loop(0, 8, widen, 0)

    for away, _ in fins:
        away.wait()


def scratch_list():
    def vm(shape, dtype=BF16):
        return pltpu.VMEM(shape, dtype)

    def weights(n):
        return vm((2, 4, 4, 2, 32, n))

    out = [vm((16, 1024), F32)] + [weights(n) for n in WIDTH] + [weights(1024)]
    out += [vm((512, 1024)), vm((512, 1024))]
    out += [vm((512, 512))] * 3
    out += [vm((8, 512, 512)), vm((512, 512))]
    out += [vm((512, 1024), F32), vm((512, 128), F32), vm((512, 1024))]
    out += [vm((512, 2048)), vm((512, 2048))]
    out += [vm((512, 1024), F32), vm((512, 1024))]
    out += [vm((512, 512)), vm((512, 1024)), vm((256, 1024))]
    out += [vm((512, 1024))] * 4 + [vm((256, 1024))]
    out += [vm((6, 8, 1024), F32), vm((3, 4, 8, 1024), F32), vm((3, 4, 8, 128), F32)]
    out += [vm((2, 8, 1024), F32), vm((2, 8, 128), F32), vm((32, 3072), F32)]
    for g, i in PIECE_LIST:
        colour, _, n = PIECES[g][i]
        out.append(vm((2, *block_dims(ORDER[colour][:2]), 16, n)))
    for g, i in PIECE_LIST:
        colour, _, n = PIECES[g][i]
        for p in range(3):
            out.append(vm((2 if p == 0 else 3, *block_dims(ORDER[colour][: 2 - p]), 32, n)))
    dma = pltpu.SemaphoreType.DMA
    out += [dma((NP, 3, 4))] * 2 + [dma((NP, 3, 5))] * 2
    out += [dma((4, 4)), dma((4, 4)), dma((6,)), dma((6,)), dma((3,))]
    out += [dma((2, 3, 3)), dma((2, 3, 3)), dma((2,)), dma((2,))]
    out += [dma((6,))] * 5
    return out


def body(
    tokens,
    w_qkv,
    b_qv,
    w_out,
    b_out,
    gain_attn,
    shift_attn,
    w_in,
    b_in,
    w_back,
    b_back,
    gain_ffn,
    shift_ffn,
    cotangent,
):
    vmem = pl.BlockSpec(memory_space=pltpu.VMEM)
    hbm = pl.BlockSpec(memory_space=pl.ANY)
    shapes = (
        jax.ShapeDtypeStruct((256, 1024), BF16),
        jax.ShapeDtypeStruct((256, 1024), F32),
        jax.ShapeDtypeStruct((3, 16, 512), F32),
        jax.ShapeDtypeStruct((16, 512), F32),
        jax.ShapeDtypeStruct((16, 2048), F32),
        jax.ShapeDtypeStruct((16, 2048), F32),
        jax.ShapeDtypeStruct((1, 2, 1024), F32),
        *(jax.ShapeDtypeStruct((1, 1024), F32) for _ in range(3)),
        jax.ShapeDtypeStruct((1, 4096), F32),
        *(jax.ShapeDtypeStruct((1, 1024), F32) for _ in range(3)),
    )
    results = pl.pallas_call(
        kernel,
        out_shape=shapes,
        in_specs=[hbm] * 6 + [vmem] * 8,
        out_specs=(hbm, *[vmem] * 13),
        scratch_shapes=scratch_list(),
        compiler_params=pltpu.CompilerParams(
            collective_id=0, has_side_effects=True, vmem_limit_bytes=60 * 1024 * 1024
        ),
        cost_estimate=pl.CostEstimate(
            flops=22_000_000_000, bytes_accessed=5_000_000, transcendentals=6_000_000
        ),
        name="encoder_layer",
    )(
        tokens,
        cotangent,
        w_qkv[0].transpose(1, 0, 2),
        w_out[0].T,
        w_in[0],
        w_back[0].T,
        b_qv,
        b_out,
        gain_attn,
        shift_attn,
        b_in,
        b_back,
        gain_ffn,
        shift_ffn,
    )

    def hand_on(*refs):
        n = len(shapes)
        ins, outs, bufs, sems = refs[:n], refs[n : 2 * n], refs[2 * n : 3 * n], refs[3 * n]
        loads = [pltpu.make_async_copy(ins[i], bufs[i], sems.at[0, i]) for i in range(n)]
        stores = [pltpu.make_async_copy(bufs[i], outs[i], sems.at[1, i]) for i in range(n)]
        for load in loads:
            load.start()
        for load, store in zip(loads, stores):
            load.wait()
            store.start()
        for store in stores:
            store.wait()

    enc, gtok, gq, go, gi, gb, d_bqv, d_bout, d_ga, d_sa, d_bin, d_bb, d_gf, d_sf = pl.pallas_call(
        hand_on,
        out_shape=shapes,
        in_specs=[hbm] * 14,
        out_specs=(hbm,) * 14,
        scratch_shapes=[*(pltpu.VMEM(t.shape, t.dtype) for t in shapes), pltpu.SemaphoreType.DMA((2, 14))],
        name="hand_on",
    )(*results)
    return (
        enc,
        gtok,
        gq.transpose(1, 0, 2)[None],
        d_bqv,
        go.T[None],
        d_bout,
        d_ga,
        d_sa,
        gi[None],
        d_bin,
        gb.T[None],
        d_bb,
        d_gf,
        d_sf,
    )


def solution(mesh):
    in_specs = (
        P(("dp", "tensor"), None),
        P(None, "dp", None, "tensor"),
        P(),
        P(None, "tensor", "dp"),
        P(),
        P(),
        P(),
        P(None, "dp", "tensor"),
        P(),
        P(None, "tensor", "dp"),
        P(),
        P(),
        P(),
        P(("dp", "tensor"), None),
    )
    out_specs = (
        P(("dp", "tensor"), None),
        P(("dp", "tensor"), None),
        P(None, "dp", None, "tensor"),
        P(),
        P(None, "tensor", "dp"),
        P(),
        P(),
        P(),
        P(None, "dp", "tensor"),
        P(),
        P(None, "tensor", "dp"),
        P(),
        P(),
        P(),
    )
    return jax.shard_map(body, mesh=mesh, in_specs=in_specs, out_specs=out_specs, check_vma=False)
```

```python
import jax
import jax.numpy as jnp
from jax import lax
from jax.experimental import pallas as pl
from jax.experimental.pallas import tpu as pltpu
from jax.sharding import PartitionSpec as P

F32 = jnp.float32
BF16 = jnp.bfloat16
MESH = pl.DeviceIdType.MESH
EPS = 1e-05
ROOT_HALF = 0.7071067811865476
INV_ROOT_TAU = 0.3989422804014327

WIDTH = (768, 256, 1024, 1024)
BASE = (0, 768, 1024, 2048)
PIECES = (
    ((0, 0, 256), (1, 256, 256), (2, 512, 256)),
    ((1, 0, 128), (2, 128, 128)),
    ((0, 0, 384), (1, 384, 384), (2, 768, 256)),
    ((0, 0, 384), (1, 384, 256), (2, 640, 384)),
)
ORDER = (("x", "z", "y"), ("z", "y", "x"), ("y", "x", "z"))
PIECE_LIST = [(g, i) for g in range(4) for i in range(len(PIECES[g]))]
SLOT = {(g, i): n for n, (g, i) in enumerate(PIECE_LIST)}
NP = len(PIECE_LIST)


def block_dims(axes_all):
    return (
        2 if "y" in axes_all else 1,
        4 if "x" in axes_all else 1,
        4 if "z" in axes_all else 1,
        2 if "y" in axes_all else 1,
    )


def dot(a, b, ca, cb):
    return lax.dot_general(a, b, (((ca,), (cb,)), ((), ())), preferred_element_type=F32)


def kernel(*refs):
    refs = list(refs)

    def take(n):
        out = refs[:n]
        del refs[:n]
        return out

    tok, cot, *raw = take(6)
    small_in = take(8)
    enc_out, gtok_out = take(2)
    gw_out = take(4)
    small_out = take(8)
    (vec,) = take(1)
    W = take(4)
    G = [None] * 4
    (G[3],) = take(1)
    G[2], G[1], G[0] = W[3], W[1], W[2]
    (X, C, Q, K, V, PR, MX, N1, INV1, H, ACT, SL, GR, GD, GM, ENC, GTR) = take(17)
    DQ, DK, DV, GTS = Q, K, V, H.at[pl.ds(0, 256)]
    S, R1, R2, R3, R4 = take(5)
    ACC, SVA, SVB, EXA, EXB, FIN = take(6)
    rs1 = take(NP)
    rs2 = take(NP * 3)
    (ag_send, ag_recv, rs_send, rs_recv, ex_send, ex_recv, io_send, io_recv, io_loc) = take(9)
    (sm_send, sm_recv, smx_send, smx_recv, pw_send, pw_recv, pw_loc, fin_send, fin_recv) = take(9)

    dp = lax.axis_index("dp")
    th = lax.axis_index("tensor")
    c = dp % 2
    yl = (dp // 2) % 2
    z = (dp // 4) % 4
    x = dp // 16
    y = th * 2 + yl
    me = {"x": x, "y": y, "z": z}

    def device(xx, yy, zz, cc):
        return (((xx * 4 + zz) * 2 + yy % 2) * 2 + cc, yy // 2)

    def nbr(axis, d):
        xx, yy, zz = x, y, z
        if axis == "x":
            xx = (x + d) % 4
        if axis == "y":
            yy = (y + d) % 4
        if axis == "z":
            zz = (z + d) % 4
        return device(xx, yy, zz, c)

    mate = device(x, y, z, 1 - c)
    partner = (((x * 4 + z) * 2 + yl) * 2 + (1 - c), 1 - th)
    stays = c == th

    def remote(src, dst, ss, rs, to):
        return pltpu.make_async_remote_copy(
            src_ref=src, dst_ref=dst, send_sem=ss, recv_sem=rs, device_id=to, device_id_type=MESH
        )

    barrier = pltpu.get_barrier_semaphore()
    talk = [nbr(a, d) for a in ("x", "y", "z") for d in (1, 2, 3)] + [mate, partner]
    for to in talk:
        pl.semaphore_signal(barrier, inc=1, device_id=to, device_id_type=MESH)
    pl.semaphore_wait(barrier, len(talk))

    def chip_rows(core):
        return pl.ds(pl.multiple_of(core * 16, 16), 16)

    def own_slot(ref, rows, cols):
        return ref.at[th, x, z, yl, rows, cols]

    RAW = [(0, j, j * 256, 256) for j in range(3)] + [(1, None, 0, 256), (2, None, 0, 1024), (3, None, 0, 1024)]

    def pw_pair(k):
        g, j, at, n = RAW[k]

        def src(t):
            cols = pl.ds(pl.multiple_of(t * n, n), n)
            return raw[g].at[j, :, cols] if g == 0 else raw[g].at[:, cols]

        dst = own_slot(W[g], chip_rows(c), pl.ds(at, n))
        away = remote(src(1 - c), dst, pw_send.at[k], pw_recv.at[k], mate)
        return away, pltpu.make_async_copy(src(c), dst, pw_loc.at[k])

    pairs = [pw_pair(k) for k in range(6)]
    for away, here in pairs:
        away.start()
        here.start()

    own_half = pl.ds(pl.multiple_of(c * 256, 256), 256)

    def swap_in(src, buf, i):
        to_partner = remote(
            src, buf.at[pl.ds(pl.multiple_of(th * 256, 256), 256)], io_send.at[i], io_recv.at[i], partner
        )
        local = pltpu.make_async_copy(src, buf.at[own_half], io_loc.at[i])
        return to_partner, local

    def to_mate(buf, i):
        return remote(buf.at[own_half], buf.at[own_half], io_send.at[2 + i], io_recv.at[2 + i], mate)

    swaps = [swap_in(tok, X, 0), swap_in(cot, C, 1)]

    def ag_block(g, i, p, coords, rows):
        colour, off, n = PIECES[g][i]
        order = ORDER[colour]
        known = order[:p]
        sel = []
        for axis in ("x", "z"):
            sel.append(pl.ds(0, 4) if axis in known else pl.ds(coords[axis], 1))
        if "y" in known:
            hs, ys = pl.ds(0, 2), pl.ds(0, 2)
        else:
            hs, ys = pl.ds(coords["y"] // 2, 1), pl.ds(coords["y"] % 2, 1)
        return W[g].at[hs, sel[0], sel[1], ys, rows, pl.ds(off, n)]

    def ag_copy(g, i, p, which):
        s = SLOT[g, i]
        axis = ORDER[PIECES[g][i][0]][p]
        at = me[axis]
        if which < 2 or p < 2:
            ref = ag_block(g, i, p, me, pl.ds(0, 32))
            to = nbr(axis, (1, 3, 2)[which])
        elif which == 2:
            ref = ag_block(g, i, p, {**me, axis: (at + 3) % 4}, pl.ds(0, 16))
            to = nbr(axis, 1)
        else:
            ref = ag_block(g, i, p, {**me, axis: (at + 1) % 4}, pl.ds(16, 16))
            to = nbr(axis, 3)
        return remote(ref, ref, ag_send.at[s, p, which], ag_recv.at[s, p, which], to)

    def ag_start(g, p):
        for i in range(len(PIECES[g])):
            for which in range(3 if p < 2 else 2):
                ag_copy(g, i, p, which).start()

    def ag_arrive(g, p):
        for i in range(len(PIECES[g])):
            for which in range(3):
                ag_copy(g, i, p, which).wait_recv()

    def ag_forward(g):
        for i in range(len(PIECES[g])):
            ag_copy(g, i, 2, 0).wait_recv()
            ag_copy(g, i, 2, 2).start()
            ag_copy(g, i, 2, 1).wait_recv()
            ag_copy(g, i, 2, 3).start()

    def ag_finish(g):
        for i in range(len(PIECES[g])):
            ag_copy(g, i, 2, 2).wait_recv()
            ag_copy(g, i, 2, 3).wait_recv()

    def ag_drain(g):
        for i in range(len(PIECES[g])):
            for p in range(3):
                for which in range(3 if p < 2 else 4):
                    ag_copy(g, i, p, which).wait_send()

    for g in range(4):
        for k in range(6):
            if RAW[k][0] == g:
                pairs[k][1].wait()
                pairs[k][0].wait()
        ag_start(g, 0)

    @pl.when(stays)
    def _():
        for a, b in swaps:
            b.start()

    @pl.when(jnp.logical_not(stays))
    def _():
        swaps[0][0].start()

    for i, ref in zip((0, 2, 3, 4, 5, 9, 10, 11), small_in):
        if i == 0:
            vec[0:2] = ref[0].astype(F32)
        elif i == 5:
            for k in range(4):
                vec[5 + k : 6 + k] = ref[:, k * 1024 : (k + 1) * 1024].astype(F32)
        else:
            vec[i : i + 1] = ref[...].astype(F32)

    for g in range(4):
        ag_arrive(g, 0)
        ag_start(g, 1)
    for g in range(2):
        ag_arrive(g, 1)
        ag_start(g, 2)

    @pl.when(stays)
    def _():
        swaps[0][1].wait()
        swaps[1][1].wait()

    @pl.when(jnp.logical_not(stays))
    def _():
        swaps[0][0].wait()
        swaps[1][0].start()

    to_mate(X, 0).start()
    ag_forward(0)
    ag_arrive(2, 1)
    ag_start(2, 2)
    ag_forward(1)
    to_mate(X, 0).wait()
    ag_finish(0)

    qkv_dst = (Q, K, V)
    lanes = lax.broadcasted_iota(jnp.int32, (1, 128), 1)

    def project(j, hh):
        w = W[0][hh, :, :, :, :, j * 256 : (j + 1) * 256].reshape(1024, 256)
        out = dot(X[...], w, 1, 0)
        if j != 1:
            row = 0 if j == 0 else 1
            start = pl.multiple_of(hh * 512 + c * 256, 256)
            out = out + vec[row : row + 1, pl.ds(start, 256)]
        out = out.astype(BF16)
        if j == 0:
            out = out * jnp.asarray(0.125, BF16)
        qkv_dst[j][:, pl.ds(pl.multiple_of(hh * 256, 256), 256)] = out

    def project_all(hh, carry):
        for j in range(3):
            project(j, hh)
        return carry

    lax.fori_loop(0, 2, project_all, 0)
    ag_arrive(3, 1)
    ag_start(3, 2)
    ag_forward(2)

    def head_mask(j):
        return (lanes < 64) if j == 0 else (lanes >= 64)

    def only(v, j):
        return jnp.where(head_mask(j), v, jnp.zeros_like(v))

    def attend(p, carry):
        cols = pl.ds(pl.multiple_of(p * 128, 128), 128)
        k2 = K[:, cols]
        v2 = V[:, cols]
        for r in range(2):
            rows = slice(r * 256, (r + 1) * 256)
            q2 = Q[rows, cols]
            acc = None
            for j in range(2):
                s = dot(only(q2, j), k2, 1, 1)
                s = jnp.exp(s - jnp.max(s, axis=-1, keepdims=True))
                s = s * (1.0 / jnp.sum(s, axis=-1, keepdims=True))
                pr = s.astype(BF16)
                PR[p * 2 + j, rows, :] = pr
                o = dot(pr, only(v2, j), 1, 0)
                acc = o if acc is None else acc + o
            MX[rows, cols] = acc.astype(BF16)
        return carry

    lax.fori_loop(0, 4, attend, 0)
    ag_finish(1)

    def ex_copy(e, dst, i):
        cols = pl.ds(pl.multiple_of(i * 256, 256), 256)
        return remote(S.at[:, cols], dst.at[:, cols], ex_send.at[e, i], ex_recv.at[e, i], mate)

    def out_part(i, carry):
        acc = None
        for hh in range(2):
            w = W[1][hh, i].reshape(256, 256)
            o = dot(MX[:, hh * 256 : (hh + 1) * 256], w, 1, 1)
            acc = o if acc is None else acc + o
        S[:, pl.ds(pl.multiple_of(i * 256, 256), 256)] = acc.astype(BF16)
        ex_copy(0, R1, i).start()
        return carry

    lax.fori_loop(0, 4, out_part, 0)
    ag_forward(3)

    def ex_wait(e, dst):
        for i in range(4):
            ex_copy(e, dst, i).wait()

    ex_wait(0, R1)

    def mean(v):
        return jnp.sum(v, axis=-1, keepdims=True) * (1.0 / 1024)

    def ln1(i, carry):
        rows = pl.ds(pl.multiple_of(i * 32, 32), 32)
        r = X[rows].astype(F32) + (S[rows].astype(F32) + R1[rows].astype(F32)) + vec[2:3]
        cen = r - mean(r)
        inv = lax.rsqrt(mean(cen * cen) + EPS)
        n = cen * inv
        N1[rows] = n
        INV1[rows] = jnp.broadcast_to(inv, (32, 128))
        H[rows] = (n * vec[3:4] + vec[4:5]).astype(BF16)
        return carry

    lax.fori_loop(0, 16, ln1, 0, unroll=2)
    ag_finish(2)

    def up(i, carry):
        cols = pl.ds(pl.multiple_of(i * 256, 256), 256)
        for hh in range(2):
            w = W[2][hh, :, :, :, :, cols].reshape(1024, 256)
            u = dot(H[...], w, 1, 0)
            u = u + vec[pl.ds(5 + hh * 2 + c, 1), cols]
            e = 0.5 * (1.0 + lax.erf(u * ROOT_HALF))
            dst = pl.ds(pl.multiple_of(hh * 1024 + i * 256, 256), 256)
            ACT[:, dst] = (u * e).astype(BF16)
            SL[:, dst] = (e + u * jnp.exp(-0.5 * u * u) * INV_ROOT_TAU).astype(BF16)
        return carry

    lax.fori_loop(0, 4, up, 0)

    @pl.when(jnp.logical_not(stays))
    def _():
        swaps[1][0].wait()

    to_mate(C, 1).start()
    ag_finish(3)

    def down(i, carry):
        acc = None
        for hh in range(2):
            w = W[3][hh, i].reshape(256, 1024)
            o = dot(ACT[:, hh * 1024 : (hh + 1) * 1024], w, 1, 1)
            acc = o if acc is None else acc + o
        S[:, pl.ds(pl.multiple_of(i * 256, 256), 256)] = acc.astype(BF16)
        ex_copy(1, R2, i).start()
        return carry

    lax.fori_loop(0, 4, down, 0)

    for g in range(4):
        ag_drain(g)
    to_mate(C, 1).wait()
    ex_wait(1, R2)

    ACC[...] = jnp.zeros_like(ACC)

    def fold(v):
        return v[0:8] + v[8:16] + (v[16:24] + v[24:32])

    def ln2(i, carry):
        rows = pl.ds(pl.multiple_of(i * 32, 32), 32)
        hidden = N1[rows] * vec[3:4] + vec[4:5]
        r = hidden + (S[rows].astype(F32) + R2[rows].astype(F32)) + vec[9:10]
        cen = r - mean(r)
        inv = lax.rsqrt(mean(cen * cen) + EPS)
        n = cen * inv
        ENC[rows] = (n * vec[10:11] + vec[11:12]).astype(BF16)
        g = C[rows].astype(F32)
        ACC[1] += fold(g * n)
        ACC[2] += fold(g)
        sc = g * vec[10:11]
        gr = inv * (sc - mean(sc) - n * mean(sc * n))
        ACC[0] += fold(gr)
        GR[rows] = gr
        GD[rows] = gr.astype(BF16)
        return carry

    lax.fori_loop(0, 16, ln2, 0, unroll=2)

    enc_local = pltpu.make_async_copy(ENC.at[own_half], enc_out, io_loc.at[2])
    enc_remote = remote(ENC.at[own_half], enc_out, io_send.at[4], io_recv.at[4], partner)

    def rs_axis(g, i, p):
        return ORDER[PIECES[g][i][0]][2 - p]

    def rs_open(g, i, p):
        return ORDER[PIECES[g][i][0]][: 2 - p]

    def rs_base(g, i, p, coord):
        opened = rs_open(g, i, p)
        at = {**me, rs_axis(g, i, p): coord}
        zero = jnp.int32(0)
        base = (
            zero if "y" in opened else at["y"] // 2,
            zero if "x" in opened else at["x"],
            zero if "z" in opened else at["z"],
            zero if "y" in opened else at["y"] % 2,
        )
        return base, block_dims(opened)

    def rs_block(g, i, p, coord, rows):
        base, dims = rs_base(g, i, p, coord)
        _, off, n = PIECES[g][i]
        return G[g].at[
            pl.ds(base[0], dims[0]),
            pl.ds(base[1], dims[1]),
            pl.ds(base[2], dims[2]),
            pl.ds(base[3], dims[3]),
            rows,
            pl.ds(off, n),
        ]

    def rs_copy(g, i, p, which):
        s = SLOT[g, i]
        axis = rs_axis(g, i, p)
        at = me[axis]
        far = (at + 2) % 4
        lower, upper = (at + 3) % 4, (at + 1) % 4
        if p == 0 and which == 0:
            src, dst, to = rs_block(g, i, p, far, pl.ds(0, 16)), rs1[s].at[0], nbr(axis, 3)
        elif p == 0 and which == 1:
            src, dst, to = rs_block(g, i, p, far, pl.ds(16, 16)), rs1[s].at[1], nbr(axis, 1)
        elif which == 2:
            src, dst, to = rs_block(g, i, p, lower, pl.ds(0, 32)), rs2[s * 3 + p].at[0], nbr(axis, 3)
        elif which == 3:
            src, dst, to = rs_block(g, i, p, upper, pl.ds(0, 32)), rs2[s * 3 + p].at[1], nbr(axis, 1)
        else:
            src, dst, to = rs_block(g, i, p, far, pl.ds(0, 32)), rs2[s * 3 + p].at[2], nbr(axis, 2)
        return remote(src, dst, rs_send.at[s, p, which], rs_recv.at[s, p, which], to)

    def unflatten(i, dims):
        out = []
        for d in reversed(dims):
            out.append(i % d if d > 1 else 0)
            i = i // d if d > 1 else i
        return tuple(reversed(out))

    def rs_mid(g, i, p, which):
        s = SLOT[g, i]
        _, off, n = PIECES[g][i]
        at = me[rs_axis(g, i, p)]
        coord = (at + 3) % 4 if which == 0 else (at + 1) % 4
        base, dims = rs_base(g, i, p, coord)
        rows = slice(which * 16, which * 16 + 16)
        buf = rs1[s]

        def one(k, carry):
            a = unflatten(k, dims)
            b = tuple(u + w for u, w in zip(base, a))
            total = G[g][(*b, rows, slice(off, off + n))].astype(F32) + buf[(which, *a)].astype(F32)
            G[g][(*b, rows, slice(off, off + n))] = total.astype(BF16)
            return carry

        lax.fori_loop(0, dims[0] * dims[1] * dims[2] * dims[3], one, 0)

    def rs_fin(g, i, p):
        s = SLOT[g, i]
        _, off, n = PIECES[g][i]
        base, dims = rs_base(g, i, p, me[rs_axis(g, i, p)])
        buf = rs2[s * 3 + p]

        def one(k, carry):
            a = unflatten(k, dims)
            b = tuple(u + w for u, w in zip(base, a))
            total = (
                G[g][(*b, slice(0, 32), slice(off, off + n))].astype(F32)
                + buf[(0, *a)].astype(F32)
                + buf[(1, *a)].astype(F32)
            )
            if p > 0:
                total = total + buf[(2, *a)].astype(F32)
            if p == 2:
                FIN[:, BASE[g] + off : BASE[g] + off + n] = total
            else:
                G[g][(*b, slice(0, 32), slice(off, off + n))] = total.astype(BF16)
            return carry

        if p == 2:
            one(0, 0)
        else:
            lax.fori_loop(0, dims[0] * dims[1] * dims[2] * dims[3], one, 0)

    def fin_pair(k):
        g, j, at, n = RAW[k]
        cols = pl.ds(pl.multiple_of(c * n, n), n)
        dst = gw_out[g].at[j, :, cols] if g == 0 else gw_out[g].at[:, cols]
        src = slice(BASE[g] + at, BASE[g] + at + n)

        def keep():
            mine = FIN[chip_rows(c), src]
            if g == 0:
                gw_out[g][j, :, cols] = mine
            else:
                gw_out[g][:, cols] = mine

        away = remote(
            FIN.at[chip_rows(1 - c), pl.ds(BASE[g] + at, n)], dst, fin_send.at[k], fin_recv.at[k], mate
        )
        return away, keep

    fins = [fin_pair(k) for k in range(6)]

    def rs_step(g, step):
        for i in range(len(PIECES[g])):
            if step == 0:
                rs_copy(g, i, 0, 0).start()
                rs_copy(g, i, 0, 1).start()
            elif step == 1:
                rs_copy(g, i, 0, 0).wait()
                rs_mid(g, i, 0, 0)
                rs_copy(g, i, 0, 2).start()
                rs_copy(g, i, 0, 1).wait()
                rs_mid(g, i, 0, 1)
                rs_copy(g, i, 0, 3).start()
            else:
                p = step - 2
                for which in (2, 3) if p == 0 else (2, 3, 4):
                    rs_copy(g, i, p, which).wait()
                rs_fin(g, i, p)
                if p < 2:
                    for which in (2, 3, 4):
                        rs_copy(g, i, p + 1, which).start()
        if step == 4:
            for k in range(6):
                if RAW[k][0] == g:
                    fins[k][0].start()
                    fins[k][1]()

    def weight_grad(g, a_ref, sources):
        def one(i, carry):
            a = a_ref[:, pl.ds(pl.multiple_of(i * 256, 256), 256)]
            for hh in range(2):
                at = 0
                for ref, starts, n in sources:
                    o = dot(a, ref[:, starts[hh] : starts[hh] + n], 0, 0)
                    G[g][hh, i, :, :, :, at : at + n] = o.astype(BF16).reshape(4, 2, 32, n)
                    at += n
            return carry

        lax.fori_loop(0, 4, one, 0)

    weight_grad(3, GD, [(ACT, (0, 1024), 1024)])
    rs_step(3, 0)

    @pl.when(stays)
    def _():
        enc_local.start()

    @pl.when(jnp.logical_not(stays))
    def _():
        enc_remote.start()

    def grad_up(i, carry):
        cols = pl.ds(pl.multiple_of(i * 256, 256), 256)
        for hh in range(2):
            w = W[3][hh, :, :, :, :, cols].reshape(1024, 256)
            dst = pl.ds(pl.multiple_of(hh * 1024 + i * 256, 256), 256)
            gu = (dot(GD[...], w, 1, 0) * SL[:, dst].astype(F32)).astype(BF16)
            SL[:, dst] = gu
            SVA[0, pl.ds(x, 1), hh : hh + 1, cols] = jnp.sum(
                gu.astype(F32), axis=0, keepdims=True
            ).reshape(1, 1, 256)
        return carry

    lax.fori_loop(0, 4, grad_up, 0)

    def hidden_part(i, carry):
        acc = None
        for hh in range(2):
            w = W[2][hh, i].reshape(256, 1024)
            o = dot(SL[:, hh * 1024 : (hh + 1) * 1024], w, 1, 1)
            acc = o if acc is None else acc + o
        S[:, pl.ds(pl.multiple_of(i * 256, 256), 256)] = acc.astype(BF16)
        ex_copy(2, R3, i).start()
        return carry

    lax.fori_loop(0, 4, hidden_part, 0)
    rs_step(3, 1)
    weight_grad(2, H, [(SL, (0, 1024), 1024)])
    rs_step(2, 0)
    ex_wait(2, R3)

    def ln1_back(i, carry):
        rows = pl.ds(pl.multiple_of(i * 32, 32), 32)
        gh = GR[rows] + (S[rows].astype(F32) + R3[rows].astype(F32))
        n = N1[rows]
        ACC[3] += fold(gh * n)
        ACC[4] += fold(gh)
        sc = gh * vec[3:4]
        inv = INV1[rows][:, 0:1]
        gr = inv * (sc - mean(sc) - n * mean(sc * n))
        ACC[5] += fold(gr)
        GR[rows] = gr
        GD[rows] = gr.astype(BF16)
        return carry

    lax.fori_loop(0, 16, ln1_back, 0, unroll=2)
    for i in range(6):
        SVA[0, pl.ds(x, 1), 2 + i : 3 + i, :] = jnp.sum(ACC[i], axis=0, keepdims=True).reshape(1, 1, 1024)

    SM_AXES = ("x", "z", "y")

    def sm_copy(buf, b, p, d):
        axis = SM_AXES[p]
        ref = buf.at[p, me[axis]]
        return remote(ref, ref, sm_send.at[b, p, d - 1], sm_recv.at[b, p, d - 1], nbr(axis, d))

    def sm_start(buf, b, p):
        for d in (1, 2, 3):
            sm_copy(buf, b, p, d).start()

    def sm_fin(buf, b, p, last):
        for d in (1, 2, 3):
            sm_copy(buf, b, p, d).wait()
        total = (buf[p, 0] + buf[p, 1]) + (buf[p, 2] + buf[p, 3])
        if p < 2:
            buf[p + 1, pl.ds(me[SM_AXES[p + 1]], 1)] = total.reshape(1, *total.shape)
        else:
            last[0] = total

    def smx_copy(ex, b):
        return remote(ex.at[0], ex.at[1], smx_send.at[b], smx_recv.at[b], mate)

    sm_start(SVA, 0, 0)

    for hh in range(2):
        w = W[1][hh].reshape(1024, 256)
        GM[:, hh * 256 : (hh + 1) * 256] = dot(GD[...], w, 1, 0).astype(BF16)
    weight_grad(1, GD, [(MX, (0, 256), 256)])
    rs_step(1, 0)

    def attend_back(p, carry):
        cols = pl.ds(pl.multiple_of(p * 128, 128), 128)
        q2 = Q[:, cols]
        k2 = K[:, cols]
        v2 = V[:, cols]
        gm2 = GM[:, cols]
        dk = None
        dq = None
        dv = None
        for j in range(2):
            gmj = only(gm2, j)
            pr = PR[p * 2 + j]
            prf = pr.astype(F32)
            gp = dot(gmj, v2, 1, 1)
            row = jnp.sum(prf * gp, axis=-1, keepdims=True)
            ds = (prf * (gp - row)).astype(BF16)
            a = dot(ds, only(k2, j), 1, 0)
            b = dot(ds, only(q2, j), 0, 0)
            e = dot(pr, gmj, 0, 0)
            dq = a if dq is None else dq + a
            dk = b if dk is None else dk + b
            dv = e if dv is None else dv + e
        dq = (dq * 0.125).astype(BF16)
        dv = dv.astype(BF16)
        DQ[:, cols] = dq
        DK[:, cols] = dk.astype(BF16)
        DV[:, cols] = dv
        SVB[0, pl.ds(x, 1), pl.ds(p, 1), :] = jnp.sum(dq.astype(F32), axis=0, keepdims=True).reshape(1, 1, 128)
        SVB[0, pl.ds(x, 1), pl.ds(4 + p, 1), :] = jnp.sum(dv.astype(F32), axis=0, keepdims=True).reshape(1, 1, 128)
        return carry

    lax.fori_loop(0, 2, attend_back, 0)
    rs_step(2, 1)
    sm_fin(SVA, 0, 0, EXA)
    sm_start(SVA, 0, 1)
    lax.fori_loop(2, 4, attend_back, 0)
    weight_grad(0, X, [(DQ, (0, 256), 256), (DK, (0, 256), 256), (DV, (0, 256), 256)])
    rs_step(0, 0)
    rs_step(1, 1)
    rs_step(3, 2)

    sm_start(SVB, 1, 0)

    other_half = pl.ds(pl.multiple_of((1 - c) * 256, 256), 256)

    def rows_part(i, carry):
        cols = pl.ds(pl.multiple_of(i * 256, 256), 256)
        acc = None
        for hh in range(2):
            for j, ref in enumerate((DQ, DK, DV)):
                w = W[0][hh, i, :, :, :, j * 256 : (j + 1) * 256].reshape(256, 256)
                o = dot(ref[:, hh * 256 : (hh + 1) * 256], w, 1, 1)
                acc = o if acc is None else acc + o
        S[:, cols] = acc.astype(BF16)
        return carry

    lax.fori_loop(0, 4, rows_part, 0)
    rows_copy = remote(S.at[other_half], R4, ex_send.at[3, 0], ex_recv.at[3, 0], mate)
    rows_copy.start()
    sm_fin(SVA, 0, 1, EXA)
    sm_start(SVA, 0, 2)
    rs_step(0, 1)
    rows_copy.wait()

    def finish(i, carry):
        here = pl.ds(pl.multiple_of(c * 256 + i * 32, 32), 32)
        rows = pl.ds(pl.multiple_of(i * 32, 32), 32)
        total = GR[here] + (S[here].astype(F32) + R4[rows].astype(F32))
        gtok_out[rows] = total
        GTS[rows] = total.astype(BF16)
        return carry

    lax.fori_loop(0, 8, finish, 0)
    gt_remote = remote(GTS, GTR, io_send.at[5], io_recv.at[5], partner)

    @pl.when(jnp.logical_not(stays))
    def _():
        gt_remote.start()

    sm_fin(SVB, 1, 0, EXB)
    sm_start(SVB, 1, 1)
    rs_step(2, 2)
    rs_step(1, 2)
    rs_step(3, 3)
    sm_fin(SVA, 0, 2, EXA)
    smx_copy(EXA, 0).start()
    rs_step(0, 2)
    sm_fin(SVB, 1, 1, EXB)
    sm_start(SVB, 1, 2)
    rs_step(2, 3)
    rs_step(1, 3)
    rs_step(3, 4)
    rs_step(0, 3)
    sm_fin(SVB, 1, 2, EXB)
    smx_copy(EXB, 1).start()
    rs_step(2, 4)
    rs_step(1, 4)
    smx_copy(EXA, 0).wait()
    smx_copy(EXB, 1).wait()
    o_bqv, o_bout, o_ga, o_sa, o_bin, o_bb, o_gf, o_sf = small_out
    first = c == 0
    own_a, oth_a = EXA[0], EXA[1]
    low_a = jnp.where(first, own_a, oth_a)
    high_a = jnp.where(first, oth_a, own_a)
    for hh in range(2):
        o_bin[:, hh * 2048 : hh * 2048 + 1024] = low_a[hh : hh + 1]
        o_bin[:, hh * 2048 + 1024 : hh * 2048 + 2048] = high_a[hh : hh + 1]
    for src, dst in ((2, o_bb), (3, o_gf), (4, o_sf), (5, o_ga), (6, o_sa), (7, o_bout)):
        dst[...] = low_a[src : src + 1]
    own_b, oth_b = EXB[0], EXB[1]
    parts_b = (jnp.where(first, own_b, oth_b), jnp.where(first, oth_b, own_b))
    for j in range(2):
        for hh in range(2):
            for cc in range(2):
                for u in range(2):
                    col = hh * 512 + cc * 256 + u * 128
                    k = j * 4 + hh * 2 + u
                    o_bqv[0, j : j + 1, col : col + 128] = parts_b[cc][k : k + 1]
    rs_step(0, 4)

    @pl.when(stays)
    def _():
        enc_local.wait()

    @pl.when(jnp.logical_not(stays))
    def _():
        enc_remote.wait()
        gt_remote.wait()

        def widen(i, carry):
            rows = pl.ds(pl.multiple_of(i * 32, 32), 32)
            gtok_out[rows] = GTR[rows].astype(F32)
            return carry

        lax.fori_loop(0, 8, widen, 0)

    for away, _ in fins:
        away.wait()


def scratch_list():
    def vm(shape, dtype=BF16):
        return pltpu.VMEM(shape, dtype)

    def weights(n):
        return vm((2, 4, 4, 2, 32, n))

    out = [vm((16, 1024), F32)] + [weights(n) for n in WIDTH] + [weights(1024)]
    out += [vm((512, 1024)), vm((512, 1024))]
    out += [vm((512, 512))] * 3
    out += [vm((8, 512, 512)), vm((512, 512))]
    out += [vm((512, 1024), F32), vm((512, 128), F32), vm((512, 1024))]
    out += [vm((512, 2048)), vm((512, 2048))]
    out += [vm((512, 1024), F32), vm((512, 1024))]
    out += [vm((512, 512)), vm((512, 1024)), vm((256, 1024))]
    out += [vm((512, 1024))] * 4 + [vm((256, 1024))]
    out += [vm((6, 8, 1024), F32), vm((3, 4, 8, 1024), F32), vm((3, 4, 8, 128), F32)]
    out += [vm((2, 8, 1024), F32), vm((2, 8, 128), F32), vm((32, 3072), F32)]
    for g, i in PIECE_LIST:
        colour, _, n = PIECES[g][i]
        out.append(vm((2, *block_dims(ORDER[colour][:2]), 16, n)))
    for g, i in PIECE_LIST:
        colour, _, n = PIECES[g][i]
        for p in range(3):
            out.append(vm((2 if p == 0 else 3, *block_dims(ORDER[colour][: 2 - p]), 32, n)))
    dma = pltpu.SemaphoreType.DMA
    out += [dma((NP, 3, 4))] * 2 + [dma((NP, 3, 5))] * 2
    out += [dma((4, 4)), dma((4, 4)), dma((6,)), dma((6,)), dma((3,))]
    out += [dma((2, 3, 3)), dma((2, 3, 3)), dma((2,)), dma((2,))]
    out += [dma((6,))] * 5
    return out


def body(
    tokens,
    w_qkv,
    b_qv,
    w_out,
    b_out,
    gain_attn,
    shift_attn,
    w_in,
    b_in,
    w_back,
    b_back,
    gain_ffn,
    shift_ffn,
    cotangent,
):
    vmem = pl.BlockSpec(memory_space=pltpu.VMEM)
    hbm = pl.BlockSpec(memory_space=pl.ANY)
    shapes = (
        jax.ShapeDtypeStruct((256, 1024), BF16),
        jax.ShapeDtypeStruct((256, 1024), F32),
        jax.ShapeDtypeStruct((3, 16, 512), F32),
        jax.ShapeDtypeStruct((16, 512), F32),
        jax.ShapeDtypeStruct((16, 2048), F32),
        jax.ShapeDtypeStruct((16, 2048), F32),
        jax.ShapeDtypeStruct((1, 2, 1024), F32),
        *(jax.ShapeDtypeStruct((1, 1024), F32) for _ in range(3)),
        jax.ShapeDtypeStruct((1, 4096), F32),
        *(jax.ShapeDtypeStruct((1, 1024), F32) for _ in range(3)),
    )
    results = pl.pallas_call(
        kernel,
        out_shape=shapes,
        in_specs=[hbm] * 6 + [vmem] * 8,
        out_specs=(hbm, *[vmem] * 13),
        scratch_shapes=scratch_list(),
        compiler_params=pltpu.CompilerParams(
            collective_id=0, has_side_effects=True, vmem_limit_bytes=60 * 1024 * 1024
        ),
        cost_estimate=pl.CostEstimate(
            flops=22_000_000_000, bytes_accessed=5_000_000, transcendentals=6_000_000
        ),
        name="encoder_layer",
    )(
        tokens,
        cotangent,
        w_qkv[0].transpose(1, 0, 2),
        w_out[0].T,
        w_in[0],
        w_back[0].T,
        b_qv,
        b_out,
        gain_attn,
        shift_attn,
        b_in,
        b_back,
        gain_ffn,
        shift_ffn,
    )

    def hand_on(*refs):
        n = len(shapes)
        ins, outs, bufs, sems = refs[:n], refs[n : 2 * n], refs[2 * n : 3 * n], refs[3 * n]
        loads = [pltpu.make_async_copy(ins[i], bufs[i], sems.at[0, i]) for i in range(n)]
        stores = [pltpu.make_async_copy(bufs[i], outs[i], sems.at[1, i]) for i in range(n)]
        for load in loads:
            load.start()
        for load, store in zip(loads, stores):
            load.wait()
            store.start()
        for store in stores:
            store.wait()

    enc, gtok, gq, go, gi, gb, d_bqv, d_bout, d_ga, d_sa, d_bin, d_bb, d_gf, d_sf = pl.pallas_call(
        hand_on,
        out_shape=shapes,
        in_specs=[hbm] * 14,
        out_specs=(hbm,) * 14,
        scratch_shapes=[*(pltpu.VMEM(t.shape, t.dtype) for t in shapes), pltpu.SemaphoreType.DMA((2, 14))],
        name="hand_on",
    )(*results)
    return (
        enc,
        gtok,
        gq.transpose(1, 0, 2)[None],
        d_bqv,
        go.T[None],
        d_bout,
        d_ga,
        d_sa,
        gi[None],
        d_bin,
        gb.T[None],
        d_bb,
        d_gf,
        d_sf,
    )


def solution(mesh):
    in_specs = (
        P(("dp", "tensor"), None),
        P(None, "dp", None, "tensor"),
        P(),
        P(None, "tensor", "dp"),
        P(),
        P(),
        P(),
        P(None, "dp", "tensor"),
        P(),
        P(None, "tensor", "dp"),
        P(),
        P(),
        P(),
        P(("dp", "tensor"), None),
    )
    out_specs = (
        P(("dp", "tensor"), None),
        P(("dp", "tensor"), None),
        P(None, "dp", None, "tensor"),
        P(),
        P(None, "tensor", "dp"),
        P(),
        P(),
        P(),
        P(None, "dp", "tensor"),
        P(),
        P(None, "tensor", "dp"),
        P(),
        P(),
        P(),
    )
    return jax.shard_map(body, mesh=mesh, in_specs=in_specs, out_specs=out_specs, check_vma=False)
```

```python
import jax
import jax.numpy as jnp
from jax import lax
from jax.experimental import pallas as pl
from jax.experimental.pallas import tpu as pltpu
from jax.sharding import PartitionSpec as P

F32 = jnp.float32
BF16 = jnp.bfloat16
MESH = pl.DeviceIdType.MESH
EPS = 1e-05
ROOT_HALF = 0.7071067811865476
INV_ROOT_TAU = 0.3989422804014327

WIDTH = (768, 256, 1024, 1024)
BASE = (0, 768, 1024, 2048)
PIECES = (
    ((0, 0, 256), (1, 256, 256), (2, 512, 256)),
    ((1, 0, 128), (2, 128, 128)),
    ((0, 0, 256), (1, 256, 384), (2, 640, 384)),
    ((0, 0, 256), (1, 256, 384), (2, 640, 384)),
)
ORDER = (("x", "z", "y"), ("z", "y", "x"), ("y", "x", "z"))
PIECE_LIST = [(g, i) for g in range(4) for i in range(len(PIECES[g]))]
SLOT = {(g, i): n for n, (g, i) in enumerate(PIECE_LIST)}
NP = len(PIECE_LIST)


def block_dims(axes_all):
    return (
        2 if "y" in axes_all else 1,
        4 if "x" in axes_all else 1,
        4 if "z" in axes_all else 1,
        2 if "y" in axes_all else 1,
    )


def dot(a, b, ca, cb):
    return lax.dot_general(a, b, (((ca,), (cb,)), ((), ())), preferred_element_type=F32)


def kernel(*refs):
    refs = list(refs)

    def take(n):
        out = refs[:n]
        del refs[:n]
        return out

    tok, cot, *raw = take(6)
    small_in = take(8)
    enc_out, gtok_out = take(2)
    gw_out = take(4)
    small_out = take(8)
    (vec,) = take(1)
    W = take(4)
    G = [None] * 4
    (G[3],) = take(1)
    G[2], G[1], G[0] = W[3], W[1], W[2]
    (X, C, Q, K, V, PR, MX, N1, INV1, H, ACT, SL, GR, GD, GM, ENC, GTR) = take(17)
    DQ, DK, DV, GTS = Q, K, V, H.at[pl.ds(0, 256)]
    S, R1, R2, R3, R4 = take(5)
    ACC, SVA, SVB, EXA, EXB, FIN = take(6)
    rs1 = take(NP)
    rs2 = take(NP * 3)
    (ag_send, ag_recv, rs_send, rs_recv, ex_send, ex_recv, io_send, io_recv, io_loc) = take(9)
    (sm_send, sm_recv, smx_send, smx_recv, pw_send, pw_recv, pw_loc, fin_send, fin_recv) = take(9)

    dp = lax.axis_index("dp")
    th = lax.axis_index("tensor")
    c = dp % 2
    yl = (dp // 2) % 2
    z = (dp // 4) % 4
    x = dp // 16
    y = th * 2 + yl
    me = {"x": x, "y": y, "z": z}

    def device(xx, yy, zz, cc):
        return (((xx * 4 + zz) * 2 + yy % 2) * 2 + cc, yy // 2)

    def nbr(axis, d):
        xx, yy, zz = x, y, z
        if axis == "x":
            xx = (x + d) % 4
        if axis == "y":
            yy = (y + d) % 4
        if axis == "z":
            zz = (z + d) % 4
        return device(xx, yy, zz, c)

    mate = device(x, y, z, 1 - c)
    partner = (((x * 4 + z) * 2 + yl) * 2 + (1 - c), 1 - th)
    stays = c == th

    def remote(src, dst, ss, rs, to):
        return pltpu.make_async_remote_copy(
            src_ref=src, dst_ref=dst, send_sem=ss, recv_sem=rs, device_id=to, device_id_type=MESH
        )

    barrier = pltpu.get_barrier_semaphore()
    talk = [nbr(a, d) for a in ("x", "y", "z") for d in (1, 2, 3)] + [mate, partner]
    for to in talk:
        pl.semaphore_signal(barrier, inc=1, device_id=to, device_id_type=MESH)
    pl.semaphore_wait(barrier, len(talk))

    def chip_rows(core):
        return pl.ds(pl.multiple_of(core * 16, 16), 16)

    def own_slot(ref, rows, cols):
        return ref.at[th, x, z, yl, rows, cols]

    RAW = [(0, j, j * 256, 256) for j in range(3)] + [(1, None, 0, 256), (2, None, 0, 1024), (3, None, 0, 1024)]

    def pw_pair(k):
        g, j, at, n = RAW[k]

        def src(t):
            cols = pl.ds(pl.multiple_of(t * n, n), n)
            return raw[g].at[j, :, cols] if g == 0 else raw[g].at[:, cols]

        dst = own_slot(W[g], chip_rows(c), pl.ds(at, n))
        away = remote(src(1 - c), dst, pw_send.at[k], pw_recv.at[k], mate)
        return away, pltpu.make_async_copy(src(c), dst, pw_loc.at[k])

    pairs = [pw_pair(k) for k in range(6)]
    for away, here in pairs:
        away.start()
        here.start()

    own_half = pl.ds(pl.multiple_of(c * 256, 256), 256)

    def swap_in(src, buf, i):
        to_partner = remote(
            src, buf.at[pl.ds(pl.multiple_of(th * 256, 256), 256)], io_send.at[i], io_recv.at[i], partner
        )
        local = pltpu.make_async_copy(src, buf.at[own_half], io_loc.at[i])
        return to_partner, local

    def to_mate(buf, i):
        return remote(buf.at[own_half], buf.at[own_half], io_send.at[2 + i], io_recv.at[2 + i], mate)

    swaps = [swap_in(tok, X, 0), swap_in(cot, C, 1)]

    def ag_block(g, i, p, coords, rows):
        colour, off, n = PIECES[g][i]
        order = ORDER[colour]
        known = order[:p]
        sel = []
        for axis in ("x", "z"):
            sel.append(pl.ds(0, 4) if axis in known else pl.ds(coords[axis], 1))
        if "y" in known:
            hs, ys = pl.ds(0, 2), pl.ds(0, 2)
        else:
            hs, ys = pl.ds(coords["y"] // 2, 1), pl.ds(coords["y"] % 2, 1)
        return W[g].at[hs, sel[0], sel[1], ys, rows, pl.ds(off, n)]

    def ag_copy(g, i, p, which):
        s = SLOT[g, i]
        axis = ORDER[PIECES[g][i][0]][p]
        at = me[axis]
        if which < 2 or p < 2:
            ref = ag_block(g, i, p, me, pl.ds(0, 32))
            to = nbr(axis, (1, 3, 2)[which])
        elif which == 2:
            ref = ag_block(g, i, p, {**me, axis: (at + 3) % 4}, pl.ds(0, 16))
            to = nbr(axis, 1)
        else:
            ref = ag_block(g, i, p, {**me, axis: (at + 1) % 4}, pl.ds(16, 16))
            to = nbr(axis, 3)
        return remote(ref, ref, ag_send.at[s, p, which], ag_recv.at[s, p, which], to)

    def ag_start(g, p):
        for i in range(len(PIECES[g])):
            for which in range(3 if p < 2 else 2):
                ag_copy(g, i, p, which).start()

    def ag_arrive(g, p):
        for i in range(len(PIECES[g])):
            for which in range(3):
                ag_copy(g, i, p, which).wait_recv()

    def ag_forward(g):
        for i in range(len(PIECES[g])):
            ag_copy(g, i, 2, 0).wait_recv()
            ag_copy(g, i, 2, 2).start()
            ag_copy(g, i, 2, 1).wait_recv()
            ag_copy(g, i, 2, 3).start()

    def ag_finish(g):
        for i in range(len(PIECES[g])):
            ag_copy(g, i, 2, 2).wait_recv()
            ag_copy(g, i, 2, 3).wait_recv()

    def ag_drain(g):
        for i in range(len(PIECES[g])):
            for p in range(3):
                for which in range(3 if p < 2 else 4):
                    ag_copy(g, i, p, which).wait_send()

    for g in range(4):
        for k in range(6):
            if RAW[k][0] == g:
                pairs[k][1].wait()
                pairs[k][0].wait()
        ag_start(g, 0)

    @pl.when(stays)
    def _():
        for a, b in swaps:
            b.start()

    @pl.when(jnp.logical_not(stays))
    def _():
        swaps[0][0].start()

    for i, ref in zip((0, 2, 3, 4, 5, 9, 10, 11), small_in):
        if i == 0:
            vec[0:2] = ref[0].astype(F32)
        elif i == 5:
            for k in range(4):
                vec[5 + k : 6 + k] = ref[:, k * 1024 : (k + 1) * 1024].astype(F32)
        else:
            vec[i : i + 1] = ref[...].astype(F32)

    for g in range(4):
        ag_arrive(g, 0)
        ag_start(g, 1)
    for g in range(2):
        ag_arrive(g, 1)
        ag_start(g, 2)

    @pl.when(stays)
    def _():
        swaps[0][1].wait()
        swaps[1][1].wait()

    @pl.when(jnp.logical_not(stays))
    def _():
        swaps[0][0].wait()
        swaps[1][0].start()

    to_mate(X, 0).start()
    ag_forward(0)
    ag_arrive(2, 1)
    ag_start(2, 2)
    ag_forward(1)
    to_mate(X, 0).wait()
    ag_finish(0)

    qkv_dst = (Q, K, V)
    lanes = lax.broadcasted_iota(jnp.int32, (1, 128), 1)

    def project(j, hh):
        w = W[0][hh, :, :, :, :, j * 256 : (j + 1) * 256].reshape(1024, 256)
        out = dot(X[...], w, 1, 0)
        if j != 1:
            row = 0 if j == 0 else 1
            start = pl.multiple_of(hh * 512 + c * 256, 256)
            out = out + vec[row : row + 1, pl.ds(start, 256)]
        out = out.astype(BF16)
        if j == 0:
            out = out * jnp.asarray(0.125, BF16)
        qkv_dst[j][:, pl.ds(pl.multiple_of(hh * 256, 256), 256)] = out

    def project_all(hh, carry):
        for j in range(3):
            project(j, hh)
        return carry

    lax.fori_loop(0, 2, project_all, 0)
    ag_arrive(3, 1)
    ag_start(3, 2)
    ag_forward(2)

    def head_mask(j):
        return (lanes < 64) if j == 0 else (lanes >= 64)

    def only(v, j):
        return jnp.where(head_mask(j), v, jnp.zeros_like(v))

    def attend(p, carry):
        cols = pl.ds(pl.multiple_of(p * 128, 128), 128)
        k2 = K[:, cols]
        v2 = V[:, cols]
        for r in range(2):
            rows = slice(r * 256, (r + 1) * 256)
            q2 = Q[rows, cols]
            acc = None
            for j in range(2):
                s = dot(only(q2, j), k2, 1, 1)
                s = jnp.exp(s - jnp.max(s, axis=-1, keepdims=True))
                s = s * (1.0 / jnp.sum(s, axis=-1, keepdims=True))
                pr = s.astype(BF16)
                PR[p * 2 + j, rows, :] = pr
                o = dot(pr, only(v2, j), 1, 0)
                acc = o if acc is None else acc + o
            MX[rows, cols] = acc.astype(BF16)
        return carry

    lax.fori_loop(0, 4, attend, 0)
    ag_finish(1)

    def ex_copy(e, dst, i):
        cols = pl.ds(pl.multiple_of(i * 256, 256), 256)
        return remote(S.at[:, cols], dst.at[:, cols], ex_send.at[e, i], ex_recv.at[e, i], mate)

    def out_part(i, carry):
        acc = None
        for hh in range(2):
            w = W[1][hh, i].reshape(256, 256)
            o = dot(MX[:, hh * 256 : (hh + 1) * 256], w, 1, 1)
            acc = o if acc is None else acc + o
        S[:, pl.ds(pl.multiple_of(i * 256, 256), 256)] = acc.astype(BF16)
        ex_copy(0, R1, i).start()
        return carry

    lax.fori_loop(0, 4, out_part, 0)
    ag_forward(3)

    def ex_wait(e, dst):
        for i in range(4):
            ex_copy(e, dst, i).wait()

    ex_wait(0, R1)

    def mean(v):
        return jnp.sum(v, axis=-1, keepdims=True) * (1.0 / 1024)

    def ln1(i, carry):
        rows = pl.ds(pl.multiple_of(i * 32, 32), 32)
        r = X[rows].astype(F32) + (S[rows].astype(F32) + R1[rows].astype(F32)) + vec[2:3]
        cen = r - mean(r)
        inv = lax.rsqrt(mean(cen * cen) + EPS)
        n = cen * inv
        N1[rows] = n
        INV1[rows] = jnp.broadcast_to(inv, (32, 128))
        H[rows] = (n * vec[3:4] + vec[4:5]).astype(BF16)
        return carry

    lax.fori_loop(0, 16, ln1, 0, unroll=2)
    ag_finish(2)

    def up(i, carry):
        cols = pl.ds(pl.multiple_of(i * 256, 256), 256)
        for hh in range(2):
            w = W[2][hh, :, :, :, :, cols].reshape(1024, 256)
            u = dot(H[...], w, 1, 0)
            u = u + vec[pl.ds(5 + hh * 2 + c, 1), cols]
            e = 0.5 * (1.0 + lax.erf(u * ROOT_HALF))
            dst = pl.ds(pl.multiple_of(hh * 1024 + i * 256, 256), 256)
            ACT[:, dst] = (u * e).astype(BF16)
            SL[:, dst] = (e + u * jnp.exp(-0.5 * u * u) * INV_ROOT_TAU).astype(BF16)
        return carry

    lax.fori_loop(0, 4, up, 0)

    @pl.when(jnp.logical_not(stays))
    def _():
        swaps[1][0].wait()

    to_mate(C, 1).start()
    ag_finish(3)

    def down(i, carry):
        acc = None
        for hh in range(2):
            w = W[3][hh, i].reshape(256, 1024)
            o = dot(ACT[:, hh * 1024 : (hh + 1) * 1024], w, 1, 1)
            acc = o if acc is None else acc + o
        S[:, pl.ds(pl.multiple_of(i * 256, 256), 256)] = acc.astype(BF16)
        ex_copy(1, R2, i).start()
        return carry

    lax.fori_loop(0, 4, down, 0)

    for g in range(4):
        ag_drain(g)
    to_mate(C, 1).wait()
    ex_wait(1, R2)

    ACC[...] = jnp.zeros_like(ACC)

    def fold(v):
        return v[0:8] + v[8:16] + (v[16:24] + v[24:32])

    def ln2(i, carry):
        rows = pl.ds(pl.multiple_of(i * 32, 32), 32)
        hidden = N1[rows] * vec[3:4] + vec[4:5]
        r = hidden + (S[rows].astype(F32) + R2[rows].astype(F32)) + vec[9:10]
        cen = r - mean(r)
        inv = lax.rsqrt(mean(cen * cen) + EPS)
        n = cen * inv
        ENC[rows] = (n * vec[10:11] + vec[11:12]).astype(BF16)
        g = C[rows].astype(F32)
        ACC[1] += fold(g * n)
        ACC[2] += fold(g)
        sc = g * vec[10:11]
        gr = inv * (sc - mean(sc) - n * mean(sc * n))
        ACC[0] += fold(gr)
        GR[rows] = gr
        GD[rows] = gr.astype(BF16)
        return carry

    lax.fori_loop(0, 16, ln2, 0, unroll=2)

    enc_local = pltpu.make_async_copy(ENC.at[own_half], enc_out, io_loc.at[2])
    enc_remote = remote(ENC.at[own_half], enc_out, io_send.at[4], io_recv.at[4], partner)

    def rs_axis(g, i, p):
        return ORDER[PIECES[g][i][0]][2 - p]

    def rs_open(g, i, p):
        return ORDER[PIECES[g][i][0]][: 2 - p]

    def rs_base(g, i, p, coord):
        opened = rs_open(g, i, p)
        at = {**me, rs_axis(g, i, p): coord}
        zero = jnp.int32(0)
        base = (
            zero if "y" in opened else at["y"] // 2,
            zero if "x" in opened else at["x"],
            zero if "z" in opened else at["z"],
            zero if "y" in opened else at["y"] % 2,
        )
        return base, block_dims(opened)

    def rs_block(g, i, p, coord, rows):
        base, dims = rs_base(g, i, p, coord)
        _, off, n = PIECES[g][i]
        return G[g].at[
            pl.ds(base[0], dims[0]),
            pl.ds(base[1], dims[1]),
            pl.ds(base[2], dims[2]),
            pl.ds(base[3], dims[3]),
            rows,
            pl.ds(off, n),
        ]

    def rs_copy(g, i, p, which):
        s = SLOT[g, i]
        axis = rs_axis(g, i, p)
        at = me[axis]
        far = (at + 2) % 4
        lower, upper = (at + 3) % 4, (at + 1) % 4
        if p == 0 and which == 0:
            src, dst, to = rs_block(g, i, p, far, pl.ds(0, 16)), rs1[s].at[0], nbr(axis, 3)
        elif p == 0 and which == 1:
            src, dst, to = rs_block(g, i, p, far, pl.ds(16, 16)), rs1[s].at[1], nbr(axis, 1)
        elif which == 2:
            src, dst, to = rs_block(g, i, p, lower, pl.ds(0, 32)), rs2[s * 3 + p].at[0], nbr(axis, 3)
        elif which == 3:
            src, dst, to = rs_block(g, i, p, upper, pl.ds(0, 32)), rs2[s * 3 + p].at[1], nbr(axis, 1)
        else:
            src, dst, to = rs_block(g, i, p, far, pl.ds(0, 32)), rs2[s * 3 + p].at[2], nbr(axis, 2)
        return remote(src, dst, rs_send.at[s, p, which], rs_recv.at[s, p, which], to)

    def unflatten(i, dims):
        out = []
        for d in reversed(dims):
            out.append(i % d if d > 1 else 0)
            i = i // d if d > 1 else i
        return tuple(reversed(out))

    def rs_mid(g, i, p, which):
        s = SLOT[g, i]
        _, off, n = PIECES[g][i]
        at = me[rs_axis(g, i, p)]
        coord = (at + 3) % 4 if which == 0 else (at + 1) % 4
        base, dims = rs_base(g, i, p, coord)
        rows = slice(which * 16, which * 16 + 16)
        buf = rs1[s]

        def one(k, carry):
            a = unflatten(k, dims)
            b = tuple(u + w for u, w in zip(base, a))
            total = G[g][(*b, rows, slice(off, off + n))].astype(F32) + buf[(which, *a)].astype(F32)
            G[g][(*b, rows, slice(off, off + n))] = total.astype(BF16)
            return carry

        lax.fori_loop(0, dims[0] * dims[1] * dims[2] * dims[3], one, 0)

    def rs_fin(g, i, p):
        s = SLOT[g, i]
        _, off, n = PIECES[g][i]
        base, dims = rs_base(g, i, p, me[rs_axis(g, i, p)])
        buf = rs2[s * 3 + p]

        def one(k, carry):
            a = unflatten(k, dims)
            b = tuple(u + w for u, w in zip(base, a))
            total = (
                G[g][(*b, slice(0, 32), slice(off, off + n))].astype(F32)
                + buf[(0, *a)].astype(F32)
                + buf[(1, *a)].astype(F32)
            )
            if p > 0:
                total = total + buf[(2, *a)].astype(F32)
            if p == 2:
                FIN[:, BASE[g] + off : BASE[g] + off + n] = total
            else:
                G[g][(*b, slice(0, 32), slice(off, off + n))] = total.astype(BF16)
            return carry

        if p == 2:
            one(0, 0)
        else:
            lax.fori_loop(0, dims[0] * dims[1] * dims[2] * dims[3], one, 0)

    def fin_pair(k):
        g, j, at, n = RAW[k]
        cols = pl.ds(pl.multiple_of(c * n, n), n)
        dst = gw_out[g].at[j, :, cols] if g == 0 else gw_out[g].at[:, cols]
        src = slice(BASE[g] + at, BASE[g] + at + n)

        def keep():
            mine = FIN[chip_rows(c), src]
            if g == 0:
                gw_out[g][j, :, cols] = mine
            else:
                gw_out[g][:, cols] = mine

        away = remote(
            FIN.at[chip_rows(1 - c), pl.ds(BASE[g] + at, n)], dst, fin_send.at[k], fin_recv.at[k], mate
        )
        return away, keep

    fins = [fin_pair(k) for k in range(6)]

    def rs_step(g, step):
        for i in range(len(PIECES[g])):
            if step == 0:
                rs_copy(g, i, 0, 0).start()
                rs_copy(g, i, 0, 1).start()
            elif step == 1:
                rs_copy(g, i, 0, 0).wait()
                rs_mid(g, i, 0, 0)
                rs_copy(g, i, 0, 2).start()
                rs_copy(g, i, 0, 1).wait()
                rs_mid(g, i, 0, 1)
                rs_copy(g, i, 0, 3).start()
            else:
                p = step - 2
                for which in (2, 3) if p == 0 else (2, 3, 4):
                    rs_copy(g, i, p, which).wait()
                rs_fin(g, i, p)
                if p < 2:
                    for which in (2, 3, 4):
                        rs_copy(g, i, p + 1, which).start()
        if step == 4:
            for k in range(6):
                if RAW[k][0] == g:
                    fins[k][0].start()
                    fins[k][1]()

    def weight_grad(g, a_ref, sources):
        def one(i, carry):
            a = a_ref[:, pl.ds(pl.multiple_of(i * 256, 256), 256)]
            for hh in range(2):
                at = 0
                for ref, starts, n in sources:
                    o = dot(a, ref[:, starts[hh] : starts[hh] + n], 0, 0)
                    G[g][hh, i, :, :, :, at : at + n] = o.astype(BF16).reshape(4, 2, 32, n)
                    at += n
            return carry

        lax.fori_loop(0, 4, one, 0)

    weight_grad(3, GD, [(ACT, (0, 1024), 1024)])
    rs_step(3, 0)

    @pl.when(stays)
    def _():
        enc_local.start()

    @pl.when(jnp.logical_not(stays))
    def _():
        enc_remote.start()

    def grad_up(i, carry):
        cols = pl.ds(pl.multiple_of(i * 256, 256), 256)
        for hh in range(2):
            w = W[3][hh, :, :, :, :, cols].reshape(1024, 256)
            dst = pl.ds(pl.multiple_of(hh * 1024 + i * 256, 256), 256)
            gu = (dot(GD[...], w, 1, 0) * SL[:, dst].astype(F32)).astype(BF16)
            SL[:, dst] = gu
            SVA[0, pl.ds(x, 1), hh : hh + 1, cols] = jnp.sum(
                gu.astype(F32), axis=0, keepdims=True
            ).reshape(1, 1, 256)
        return carry

    lax.fori_loop(0, 4, grad_up, 0)

    def hidden_part(i, carry):
        acc = None
        for hh in range(2):
            w = W[2][hh, i].reshape(256, 1024)
            o = dot(SL[:, hh * 1024 : (hh + 1) * 1024], w, 1, 1)
            acc = o if acc is None else acc + o
        S[:, pl.ds(pl.multiple_of(i * 256, 256), 256)] = acc.astype(BF16)
        ex_copy(2, R3, i).start()
        return carry

    lax.fori_loop(0, 4, hidden_part, 0)
    rs_step(3, 1)
    weight_grad(2, H, [(SL, (0, 1024), 1024)])
    rs_step(2, 0)
    ex_wait(2, R3)

    def ln1_back(i, carry):
        rows = pl.ds(pl.multiple_of(i * 32, 32), 32)
        gh = GR[rows] + (S[rows].astype(F32) + R3[rows].astype(F32))
        n = N1[rows]
        ACC[3] += fold(gh * n)
        ACC[4] += fold(gh)
        sc = gh * vec[3:4]
        inv = INV1[rows][:, 0:1]
        gr = inv * (sc - mean(sc) - n * mean(sc * n))
        ACC[5] += fold(gr)
        GR[rows] = gr
        GD[rows] = gr.astype(BF16)
        return carry

    lax.fori_loop(0, 16, ln1_back, 0, unroll=2)
    for i in range(6):
        SVA[0, pl.ds(x, 1), 2 + i : 3 + i, :] = jnp.sum(ACC[i], axis=0, keepdims=True).reshape(1, 1, 1024)

    SM_AXES = ("x", "z", "y")

    def sm_copy(buf, b, p, d):
        axis = SM_AXES[p]
        ref = buf.at[p, me[axis]]
        return remote(ref, ref, sm_send.at[b, p, d - 1], sm_recv.at[b, p, d - 1], nbr(axis, d))

    def sm_start(buf, b, p):
        for d in (1, 2, 3):
            sm_copy(buf, b, p, d).start()

    def sm_fin(buf, b, p, last):
        for d in (1, 2, 3):
            sm_copy(buf, b, p, d).wait()
        total = (buf[p, 0] + buf[p, 1]) + (buf[p, 2] + buf[p, 3])
        if p < 2:
            buf[p + 1, pl.ds(me[SM_AXES[p + 1]], 1)] = total.reshape(1, *total.shape)
        else:
            last[0] = total

    def smx_copy(ex, b):
        return remote(ex.at[0], ex.at[1], smx_send.at[b], smx_recv.at[b], mate)

    sm_start(SVA, 0, 0)

    for hh in range(2):
        w = W[1][hh].reshape(1024, 256)
        GM[:, hh * 256 : (hh + 1) * 256] = dot(GD[...], w, 1, 0).astype(BF16)
    weight_grad(1, GD, [(MX, (0, 256), 256)])
    rs_step(1, 0)

    def attend_back(p, carry):
        cols = pl.ds(pl.multiple_of(p * 128, 128), 128)
        q2 = Q[:, cols]
        k2 = K[:, cols]
        v2 = V[:, cols]
        gm2 = GM[:, cols]
        dk = None
        dq = None
        dv = None
        for j in range(2):
            gmj = only(gm2, j)
            pr = PR[p * 2 + j]
            prf = pr.astype(F32)
            gp = dot(gmj, v2, 1, 1)
            row = jnp.sum(prf * gp, axis=-1, keepdims=True)
            ds = (prf * (gp - row)).astype(BF16)
            a = dot(ds, only(k2, j), 1, 0)
            b = dot(ds, only(q2, j), 0, 0)
            e = dot(pr, gmj, 0, 0)
            dq = a if dq is None else dq + a
            dk = b if dk is None else dk + b
            dv = e if dv is None else dv + e
        dq = (dq * 0.125).astype(BF16)
        dv = dv.astype(BF16)
        DQ[:, cols] = dq
        DK[:, cols] = dk.astype(BF16)
        DV[:, cols] = dv
        SVB[0, pl.ds(x, 1), pl.ds(p, 1), :] = jnp.sum(dq.astype(F32), axis=0, keepdims=True).reshape(1, 1, 128)
        SVB[0, pl.ds(x, 1), pl.ds(4 + p, 1), :] = jnp.sum(dv.astype(F32), axis=0, keepdims=True).reshape(1, 1, 128)
        return carry

    lax.fori_loop(0, 2, attend_back, 0)
    rs_step(2, 1)
    sm_fin(SVA, 0, 0, EXA)
    sm_start(SVA, 0, 1)
    lax.fori_loop(2, 4, attend_back, 0)
    weight_grad(0, X, [(DQ, (0, 256), 256), (DK, (0, 256), 256), (DV, (0, 256), 256)])
    rs_step(0, 0)
    rs_step(1, 1)
    rs_step(3, 2)

    sm_start(SVB, 1, 0)

    other_half = pl.ds(pl.multiple_of((1 - c) * 256, 256), 256)

    def rows_part(i, carry):
        cols = pl.ds(pl.multiple_of(i * 256, 256), 256)
        acc = None
        for hh in range(2):
            for j, ref in enumerate((DQ, DK, DV)):
                w = W[0][hh, i, :, :, :, j * 256 : (j + 1) * 256].reshape(256, 256)
                o = dot(ref[:, hh * 256 : (hh + 1) * 256], w, 1, 1)
                acc = o if acc is None else acc + o
        S[:, cols] = acc.astype(BF16)
        return carry

    lax.fori_loop(0, 4, rows_part, 0)
    rows_copy = remote(S.at[other_half], R4, ex_send.at[3, 0], ex_recv.at[3, 0], mate)
    rows_copy.start()
    sm_fin(SVA, 0, 1, EXA)
    sm_start(SVA, 0, 2)
    rs_step(0, 1)
    rows_copy.wait()

    def finish(i, carry):
        here = pl.ds(pl.multiple_of(c * 256 + i * 32, 32), 32)
        rows = pl.ds(pl.multiple_of(i * 32, 32), 32)
        total = GR[here] + (S[here].astype(F32) + R4[rows].astype(F32))
        gtok_out[rows] = total
        GTS[rows] = total.astype(BF16)
        return carry

    lax.fori_loop(0, 8, finish, 0)
    gt_remote = remote(GTS, GTR, io_send.at[5], io_recv.at[5], partner)

    @pl.when(jnp.logical_not(stays))
    def _():
        gt_remote.start()

    sm_fin(SVB, 1, 0, EXB)
    sm_start(SVB, 1, 1)
    rs_step(2, 2)
    rs_step(1, 2)
    rs_step(3, 3)
    sm_fin(SVA, 0, 2, EXA)
    smx_copy(EXA, 0).start()
    rs_step(0, 2)
    sm_fin(SVB, 1, 1, EXB)
    sm_start(SVB, 1, 2)
    rs_step(2, 3)
    rs_step(1, 3)
    rs_step(3, 4)
    rs_step(0, 3)
    sm_fin(SVB, 1, 2, EXB)
    smx_copy(EXB, 1).start()
    rs_step(2, 4)
    rs_step(1, 4)
    smx_copy(EXA, 0).wait()
    smx_copy(EXB, 1).wait()
    o_bqv, o_bout, o_ga, o_sa, o_bin, o_bb, o_gf, o_sf = small_out
    first = c == 0
    own_a, oth_a = EXA[0], EXA[1]
    low_a = jnp.where(first, own_a, oth_a)
    high_a = jnp.where(first, oth_a, own_a)
    for hh in range(2):
        o_bin[:, hh * 2048 : hh * 2048 + 1024] = low_a[hh : hh + 1]
        o_bin[:, hh * 2048 + 1024 : hh * 2048 + 2048] = high_a[hh : hh + 1]
    for src, dst in ((2, o_bb), (3, o_gf), (4, o_sf), (5, o_ga), (6, o_sa), (7, o_bout)):
        dst[...] = low_a[src : src + 1]
    own_b, oth_b = EXB[0], EXB[1]
    parts_b = (jnp.where(first, own_b, oth_b), jnp.where(first, oth_b, own_b))
    for j in range(2):
        for hh in range(2):
            for cc in range(2):
                for u in range(2):
                    col = hh * 512 + cc * 256 + u * 128
                    k = j * 4 + hh * 2 + u
                    o_bqv[0, j : j + 1, col : col + 128] = parts_b[cc][k : k + 1]
    rs_step(0, 4)

    @pl.when(stays)
    def _():
        enc_local.wait()

    @pl.when(jnp.logical_not(stays))
    def _():
        enc_remote.wait()
        gt_remote.wait()

        def widen(i, carry):
            rows = pl.ds(pl.multiple_of(i * 32, 32), 32)
            gtok_out[rows] = GTR[rows].astype(F32)
            return carry

        lax.fori_loop(0, 8, widen, 0)

    for away, _ in fins:
        away.wait()


def scratch_list():
    def vm(shape, dtype=BF16):
        return pltpu.VMEM(shape, dtype)

    def weights(n):
        return vm((2, 4, 4, 2, 32, n))

    out = [vm((16, 1024), F32)] + [weights(n) for n in WIDTH] + [weights(1024)]
    out += [vm((512, 1024)), vm((512, 1024))]
    out += [vm((512, 512))] * 3
    out += [vm((8, 512, 512)), vm((512, 512))]
    out += [vm((512, 1024), F32), vm((512, 128), F32), vm((512, 1024))]
    out += [vm((512, 2048)), vm((512, 2048))]
    out += [vm((512, 1024), F32), vm((512, 1024))]
    out += [vm((512, 512)), vm((512, 1024)), vm((256, 1024))]
    out += [vm((512, 1024))] * 4 + [vm((256, 1024))]
    out += [vm((6, 8, 1024), F32), vm((3, 4, 8, 1024), F32), vm((3, 4, 8, 128), F32)]
    out += [vm((2, 8, 1024), F32), vm((2, 8, 128), F32), vm((32, 3072), F32)]
    for g, i in PIECE_LIST:
        colour, _, n = PIECES[g][i]
        out.append(vm((2, *block_dims(ORDER[colour][:2]), 16, n)))
    for g, i in PIECE_LIST:
        colour, _, n = PIECES[g][i]
        for p in range(3):
            out.append(vm((2 if p == 0 else 3, *block_dims(ORDER[colour][: 2 - p]), 32, n)))
    dma = pltpu.SemaphoreType.DMA
    out += [dma((NP, 3, 4))] * 2 + [dma((NP, 3, 5))] * 2
    out += [dma((4, 4)), dma((4, 4)), dma((6,)), dma((6,)), dma((3,))]
    out += [dma((2, 3, 3)), dma((2, 3, 3)), dma((2,)), dma((2,))]
    out += [dma((6,))] * 5
    return out


def body(
    tokens,
    w_qkv,
    b_qv,
    w_out,
    b_out,
    gain_attn,
    shift_attn,
    w_in,
    b_in,
    w_back,
    b_back,
    gain_ffn,
    shift_ffn,
    cotangent,
):
    vmem = pl.BlockSpec(memory_space=pltpu.VMEM)
    hbm = pl.BlockSpec(memory_space=pl.ANY)
    shapes = (
        jax.ShapeDtypeStruct((256, 1024), BF16),
        jax.ShapeDtypeStruct((256, 1024), F32),
        jax.ShapeDtypeStruct((3, 16, 512), F32),
        jax.ShapeDtypeStruct((16, 512), F32),
        jax.ShapeDtypeStruct((16, 2048), F32),
        jax.ShapeDtypeStruct((16, 2048), F32),
        jax.ShapeDtypeStruct((1, 2, 1024), F32),
        *(jax.ShapeDtypeStruct((1, 1024), F32) for _ in range(3)),
        jax.ShapeDtypeStruct((1, 4096), F32),
        *(jax.ShapeDtypeStruct((1, 1024), F32) for _ in range(3)),
    )
    results = pl.pallas_call(
        kernel,
        out_shape=shapes,
        in_specs=[hbm] * 6 + [vmem] * 8,
        out_specs=(hbm, *[vmem] * 13),
        scratch_shapes=scratch_list(),
        compiler_params=pltpu.CompilerParams(
            collective_id=0, has_side_effects=True, vmem_limit_bytes=60 * 1024 * 1024
        ),
        cost_estimate=pl.CostEstimate(
            flops=22_000_000_000, bytes_accessed=5_000_000, transcendentals=6_000_000
        ),
        name="encoder_layer",
    )(
        tokens,
        cotangent,
        w_qkv[0].transpose(1, 0, 2),
        w_out[0].T,
        w_in[0],
        w_back[0].T,
        b_qv,
        b_out,
        gain_attn,
        shift_attn,
        b_in,
        b_back,
        gain_ffn,
        shift_ffn,
    )

    def hand_on(*refs):
        n = len(shapes)
        ins, outs, bufs, sems = refs[:n], refs[n : 2 * n], refs[2 * n : 3 * n], refs[3 * n]
        loads = [pltpu.make_async_copy(ins[i], bufs[i], sems.at[0, i]) for i in range(n)]
        stores = [pltpu.make_async_copy(bufs[i], outs[i], sems.at[1, i]) for i in range(n)]
        for load in loads:
            load.start()
        for load, store in zip(loads, stores):
            load.wait()
            store.start()
        for store in stores:
            store.wait()

    enc, gtok, gq, go, gi, gb, d_bqv, d_bout, d_ga, d_sa, d_bin, d_bb, d_gf, d_sf = pl.pallas_call(
        hand_on,
        out_shape=shapes,
        in_specs=[hbm] * 14,
        out_specs=(hbm,) * 14,
        scratch_shapes=[*(pltpu.VMEM(t.shape, t.dtype) for t in shapes), pltpu.SemaphoreType.DMA((2, 14))],
        name="hand_on",
    )(*results)
    return (
        enc,
        gtok,
        gq.transpose(1, 0, 2)[None],
        d_bqv,
        go.T[None],
        d_bout,
        d_ga,
        d_sa,
        gi[None],
        d_bin,
        gb.T[None],
        d_bb,
        d_gf,
        d_sf,
    )


def solution(mesh):
    in_specs = (
        P(("dp", "tensor"), None),
        P(None, "dp", None, "tensor"),
        P(),
        P(None, "tensor", "dp"),
        P(),
        P(),
        P(),
        P(None, "dp", "tensor"),
        P(),
        P(None, "tensor", "dp"),
        P(),
        P(),
        P(),
        P(("dp", "tensor"), None),
    )
    out_specs = (
        P(("dp", "tensor"), None),
        P(("dp", "tensor"), None),
        P(None, "dp", None, "tensor"),
        P(),
        P(None, "tensor", "dp"),
        P(),
        P(),
        P(),
        P(None, "dp", "tensor"),
        P(),
        P(None, "tensor", "dp"),
        P(),
        P(),
        P(),
    )
    return jax.shard_map(body, mesh=mesh, in_specs=in_specs, out_specs=out_specs, check_vma=False)
```
